512 devices in a mesh: freq: 16 (over y_hi, x, core), grid: 32 (over y_lo, z).
Axes of the slice: x: 4, y: 4 (y_hi: 2, y_lo: 2; y = y_hi * 2 + y_lo), z: 16, core: 2. Of those that a mesh axis runs over, the one named last changes fastest.
Arguments:
- series: bfloat16 [512, 1024, 256], P('freq', 'grid'), may hold values from -8 to 8
- bins: int32 [16], replicated, may hold values from 32 to 127
- sensor_coords: int32 [3, 1024], replicated, may hold values from 0 to 63
- grid_coords: int32 [3, 8192], P(None, 'grid'), may hold values from 0 to 63
Outputs:
- bin_power: float32 [16, 8192], P('freq', 'grid')
- power: float32 [8192], P('grid')
The draws below stay inside these ranges and needn't reach their ends.
All inputs are finite; a program needn't handle non-finite values.
Results may differ from the reference program's by a relative error of at most 0.0015.
Values may be sent and summed in bfloat16 or wider, within the bound.
A program may use at most 64 MiB of HBM per device.

```python
import math
import jax
import jax.numpy as jnp
from jax import lax

CH = 1024
SAMP = 256
COORD = 64
NF = 16
SNAPS = 512
GRID = 8192


def draw_series(key, part):
    keys = jax.random.split(jax.random.fold_in(key, 11), 4)
    loud = 16
    lowest, highest = (0.12, 0.4)
    noise = jax.random.normal(keys[0], (SNAPS, CH, SAMP), jnp.float32)
    waves = jax.random.normal(keys[1], (SNAPS, loud, SAMP), jnp.float32)
    mixing = jax.random.normal(keys[2], (CH, loud), jnp.float32)
    levels = jnp.exp(jax.random.uniform(keys[3], (loud,), jnp.float32, jnp.log(lowest), jnp.log(highest)))
    signal = jnp.einsum('skt,ck->sct', waves * levels[None, :, None], mixing)
    return jnp.clip((noise + signal) / 2.0, -8.0, 8.0).astype(jnp.bfloat16)


def touch_ends(result, stream_key, least, high):
    extent = result.shape
    index_at = [jax.random.randint(jax.random.fold_in(stream_key, axis), (), 0, extent[axis]) for axis in range(len(extent))]
    result = result.at[tuple(index_at)].set(least)
    longest = extent.index(max(extent))
    index_at[longest] = (index_at[longest] + 1) % extent[longest]
    return result.at[tuple(index_at)].set(high)


def setup_inputs(seed: int = 0) -> dict:
    streams_of = jax.random.split(jax.random.key(seed), 5)
    return {
        "series": draw_series(jax.random.fold_in(streams_of[4], 71), 0),
        "bins": touch_ends(jax.random.randint(streams_of[1], (NF,), SAMP // 8, SAMP // 2), jax.random.fold_in(streams_of[1], 1), SAMP // 8, (SAMP // 2) - 1).astype(jnp.int32),
        "sensor_coords": touch_ends(jax.random.randint(streams_of[2], (3, CH), 0, COORD), jax.random.fold_in(streams_of[2], 1), 0, COORD - 1).astype(jnp.int32),
        "grid_coords": touch_ends(jax.random.randint(streams_of[3], (3, GRID), 0, COORD), jax.random.fold_in(streams_of[3], 1), 0, COORD - 1).astype(jnp.int32),
    }


def make_table(bins, samples):
    sample_index = jnp.arange(samples, dtype=jnp.int32)
    cycles = bins[:, None] * sample_index[None, :] % samples
    angles = 2.0 * math.pi / samples * cycles.astype(jnp.float32)
    scaling = (samples / 2.0) ** (-0.5)
    table = jnp.stack([jnp.cos(angles) * scaling, -jnp.sin(angles) * scaling], 1)
    return table.astype(jnp.bfloat16).reshape(2 * bins.shape[0], samples)

def reference(series, bins, sensor_coords, grid_coords):
    snap_total, channels, samples = series.shape
    table = make_table(bins, samples)
    flat = series.reshape(snap_total * channels, samples)
    spectra = jnp.dot(table, flat.T, preferred_element_type=jnp.float32)
    spectra = spectra.astype(jnp.bfloat16).reshape(2 * bins.shape[0], snap_total, channels)
    spectra = jnp.transpose(spectra, (0, 2, 1)).reshape(bins.shape[0], 2, channels, snap_total)
    squared = jnp.zeros((grid_coords.shape[1], channels), jnp.int32)
    for axis_pos in range(3):
        offsets = grid_coords[axis_pos][:, None] - sensor_coords[axis_pos][None, :]
        squared = squared + offsets * offsets
    distance = jnp.sqrt(squared.astype(jnp.float32))
    amplitude = channels ** (-0.5)

    def one_bin(item):
        bin_value, spec = item
        phases = 4.0 * math.pi / samples * bin_value.astype(jnp.float32) * distance
        beam_real = (jnp.cos(phases) * amplitude).astype(jnp.bfloat16).astype(jnp.float32)
        beam_imag = (-jnp.sin(phases) * amplitude).astype(jnp.bfloat16).astype(jnp.float32)
        spec_real = spec[0].astype(jnp.float32)
        spec_imag = spec[1].astype(jnp.float32)
        out_real = jnp.dot(beam_real, spec_real) + jnp.dot(beam_imag, spec_imag)
        out_imag = jnp.dot(beam_real, spec_imag) - jnp.dot(beam_imag, spec_real)
        return lax.optimization_barrier(jnp.sum(out_real * out_real + out_imag * out_imag, 1)) / snap_total
    bin_power = lax.map(one_bin, (bins, spectra))
    power = lax.optimization_barrier(jnp.sum(bin_power, 0)) / bins.shape[0]
    return (bin_power, power)
```

```python
import jax
import jax.numpy as jnp
from jax import lax
from jax.experimental import pallas as pl
from jax.experimental.pallas import tpu as pltpu
from jax.sharding import PartitionSpec as P

MESH = pl.DeviceIdType.MESH

SIN_COEF = (4.442883014678955, -7.308245658874512, 3.606354236602783, -0.8461116552352905, 0.1098245158791542)
COS_COEF = (1.4142135381698608, -6.978850841522217, 5.739460468292236, -1.883557915687561, 0.3106880187988281)

XS, ZS, BINS = 4, 16, 16
CH_LOC, SNAP_LOC, SAMP, BLOCK = 32, 32, 256, 256
CH = 1024


def horner(coef, z):
    acc = coef[-1] * z + coef[-2]
    for value in coef[-3::-1]:
        acc = acc * z + value
    return acc


def sincos_turns(turns):
    r = turns - jnp.round(turns)
    z = r * r
    s = horner(SIN_COEF, z) * r
    c = horner(COS_COEF, z)
    return 1.0 - s * s, s * c


def kernel(
    bins_ref, sensor_ref, grid_ref, series_ref, bin_power_ref, power_ref,
    series_v, table_v, sensors_t, points_own, points, spec_f32, send1, recv1, slots, turned, wave_c, wave_s,
    part, recv3, stage, recv4,
    series_sem, points_send, points_recv, send1_sem, recv1_sem, send2_sem, recv2_sem,
    send3_sem, recv3_sem, send4_sem, recv4_sem,
):
    f = lax.axis_index("freq")
    g = lax.axis_index("grid")
    core, x, y_hi = lax.rem(f, 2), lax.rem(f // 2, XS), f // (2 * XS)
    z, y_lo = lax.rem(g, ZS), g // ZS
    fpos = y_hi * 2 + core
    own8 = fpos * 2 + y_lo

    def plane_partner(k):
        other = lax.rem(own8 + k, 8)
        lo, pos = lax.rem(other, 2), other // 2
        return ((pos // 2) * (2 * XS) + x * 2 + lax.rem(pos, 2), lo * ZS + z)

    def x_partner(k):
        xo = lax.rem(x + k, XS)
        return xo, (y_hi * (2 * XS) + xo * 2 + core, g)

    def z_partner(k):
        zo = lax.rem(z + k, ZS)
        return zo, (f, y_lo * ZS + zo)

    load = pltpu.make_async_copy(series_ref, series_v, series_sem)
    load.start()

    barrier = pltpu.get_barrier_semaphore()
    for k in range(1, ZS):
        pl.semaphore_signal(barrier, inc=1, device_id=z_partner(k)[1], device_id_type=MESH)
    for k in range(1, 8):
        pl.semaphore_signal(barrier, inc=1, device_id=plane_partner(k), device_id_type=MESH)
    for k in range(1, XS):
        pl.semaphore_signal(barrier, inc=1, device_id=x_partner(k)[1], device_id_type=MESH)

    def lattice(coords, flip):
        c = coords.astype(jnp.float32)
        norm = jnp.sum(c * c, axis=0, keepdims=True)
        high = jnp.floor(norm * (1.0 / 128.0)) * 128.0
        low = norm - high
        one = jnp.ones_like(norm)
        tail = (high, low, one, one) if flip else (one, one, high, low)
        scale = 1.0 if flip else -2.0
        zeros = jnp.zeros((9, c.shape[1]), jnp.float32)
        return jnp.concatenate([c * scale, *tail, zeros], axis=0)

    points_own[...] = lattice(grid_ref[...], False).astype(jnp.bfloat16)

    row = lax.broadcasted_iota(jnp.int32, (2 * BINS, SAMP), 0)
    time = lax.broadcasted_iota(jnp.int32, (2 * BINS, SAMP), 1)
    number = jnp.zeros((2 * BINS, SAMP), jnp.int32)
    for b in range(BINS):
        number = jnp.where(row // 2 == b, bins_ref[b], number)
    cycles = (number * time + (row % 2) * (SAMP // 4)) & (SAMP - 1)
    table_v[...] = (sincos_turns(cycles.astype(jnp.float32) * (1.0 / SAMP))[0] * (SAMP / 2.0) ** -0.5).astype(
        jnp.bfloat16
    )

    pl.semaphore_wait(barrier, ZS - 1 + 7 + XS - 1)

    mine = lax.rem(z, 4)

    @pl.when(z // 4 == fpos)
    def _():
        for k in range(1, ZS):
            pltpu.make_async_remote_copy(
                points_own, points.at[mine], points_send, points_recv,
                device_id=z_partner(k)[1], device_id_type=MESH,
            ).start()
        pltpu.make_async_copy(points_own, points.at[mine], points_recv).start()

    load.wait()
    spec = lax.dot_general(
        table_v[...], series_v[...].reshape(SNAP_LOC * CH_LOC, SAMP),
        (((1,), (1,)), ((), ())), preferred_element_type=jnp.float32,
    )
    for t in range(8):
        spec_f32[:, t, :] = spec[:, t * 128:(t + 1) * 128]
    send1[...] = spec_f32[...].reshape(BINS, 16, 128).astype(jnp.bfloat16)
    for k in range(1, ZS):
        zo, device = z_partner(k)
        pltpu.make_async_remote_copy(
            send1.at[zo], recv1.at[z], send1_sem, recv1_sem, device_id=device, device_id_type=MESH
        ).start()
    pltpu.make_async_copy(send1.at[z], recv1.at[z], recv1_sem).start()

    sensors_t[...] = jnp.transpose(
        jnp.concatenate([lattice(sensor_ref[...], True), jnp.zeros((112, CH), jnp.float32)], axis=0)
    ).astype(jnp.bfloat16)

    pltpu.make_async_copy(points, points, points_recv).wait()

    rate = bins_ref[z].astype(jnp.float32) * (1.0 / 128.0)

    def replicas(j):
        rhs = points[j]

        def body(i, carry):
            rows = pl.ds(pl.multiple_of(i * 128, 128), 128)
            squared = jnp.dot(sensors_t[rows, :16], rhs, preferred_element_type=jnp.float32)
            root = lax.rsqrt(jnp.maximum(squared, 0.5))
            c, s = sincos_turns((squared * rate) * root)
            wave_c[j, rows, :] = c.astype(jnp.bfloat16)
            wave_s[j, rows, :] = s.astype(jnp.bfloat16)
            return carry

        lax.fori_loop(0, CH // 128, body, 0)

    replicas(0)

    pltpu.make_async_copy(recv1, recv1, recv1_sem).wait()
    lane = lax.broadcasted_iota(jnp.int32, (16, 128), 1) // 32
    for q in range(4):
        pieces = [recv1[4 * q + j].astype(jnp.float32) for j in range(4)]
        tiles = []
        for h in range(4):
            tile = None
            for j in range(4):
                shift = ((j - h) * 32) % 128
                moved = pieces[j] if shift == 0 else pltpu.roll(pieces[j], shift, 1)
                tile = moved if tile is None else jnp.where(lane == j, moved, tile)
            tiles.append(tile)
        stacked = jnp.concatenate([t[:8] for t in tiles] + [t[8:] for t in tiles], axis=0)
        slots[own8, :, q * 128:(q + 1) * 128] = stacked.astype(jnp.bfloat16)
    for k in range(1, 8):
        pltpu.make_async_remote_copy(
            slots.at[own8], slots.at[own8], send2_sem, recv2_sem.at[own8],
            device_id=plane_partner(k), device_id_type=MESH,
        ).start()

    for j in range(1, 4):
        replicas(j)

    def turn(slot):
        turned[slot, :32] = -slots[slot, 32:]
        turned[slot, 32:] = slots[slot, :32]

    turn(own8)
    for k in range(1, 8):
        other = lax.rem(own8 + 8 - k, 8)
        pltpu.make_async_copy(slots.at[other], slots.at[other], recv2_sem.at[other]).wait()
        turn(other)

    def beam(j):
        acc = None
        for lo in range(2):
            direct = jnp.concatenate([slots[2 * p + lo] for p in range(4)], axis=0)
            crossed = jnp.concatenate([turned[2 * p + lo] for p in range(4)], axis=0)
            rows = pl.ds(lo * 512, 512)
            term = jnp.dot(direct, wave_c[j, rows, :], preferred_element_type=jnp.float32)
            term = term + jnp.dot(crossed, wave_s[j, rows, :], preferred_element_type=jnp.float32)
            acc = term if acc is None else acc + term
        return jnp.sum(acc * acc, axis=0, keepdims=True) * (1.0 / (512.0 * 1024.0))

    for k in range(1, XS):
        xo, device = x_partner(k)
        part[xo] = beam(xo)
        pltpu.make_async_remote_copy(
            part.at[xo], recv3.at[x], send3_sem, recv3_sem, device_id=device, device_id_type=MESH
        ).start()
    total = beam(x)
    recv3[x] = total
    pltpu.make_async_copy(recv3.at[0:3], recv3.at[0:3], recv3_sem).wait()
    stage[...] = (recv3[0] + recv3[1]) + (recv3[2] + recv3[3])

    owner = 4 * fpos + x
    home = owner == z
    for k in range(BINS):
        fo = lax.rem(f + k, BINS)

        def send():
            pltpu.make_async_remote_copy(
                stage, recv4.at[z], send4_sem, recv4_sem, device_id=(fo, y_lo * ZS + owner), device_id_type=MESH
            ).start()

        if k > 0:
            send()
        else:
            pl.when(jnp.logical_not(home))(send)

            @pl.when(home)
            def _():
                pltpu.make_async_copy(stage, recv4.at[z], recv4_sem).start()

    pltpu.make_async_copy(recv4, recv4, recv4_sem).wait()
    bin_power_ref[...] = recv4[f]
    total = recv4[0]
    for b in range(1, BINS):
        total = total + recv4[b]
    power_ref[...] = total * (1.0 / BINS)

    @pl.when(z // 4 == fpos)
    def _():
        sent = wave_c.at[0, 0:15 * 16]
        pltpu.make_async_copy(sent, sent, points_send).wait()

    pltpu.make_async_copy(send1.at[0:15], send1.at[0:15], send1_sem).wait()
    pltpu.make_async_copy(slots.at[0:7], slots.at[0:7], send2_sem).wait()
    pltpu.make_async_copy(part.at[0:3], part.at[0:3], send3_sem).wait()
    pltpu.make_async_copy(recv4.at[0:15], recv4.at[0:15], send4_sem).wait()

    @pl.when(jnp.logical_not(home))
    def _():
        pltpu.make_async_copy(stage, stage, send4_sem).wait()


def on_device(series, bins, sensor_coords, grid_coords):
    vmem = pltpu.VMEM
    bf16, f32 = jnp.bfloat16, jnp.float32
    dma = pltpu.SemaphoreType.DMA
    bin_power, power = pl.pallas_call(
        kernel,
        out_shape=(jax.ShapeDtypeStruct((1, BLOCK), f32), jax.ShapeDtypeStruct((1, BLOCK), f32)),
        in_specs=[
            pl.BlockSpec(memory_space=pltpu.SMEM),
            pl.BlockSpec(memory_space=vmem),
            pl.BlockSpec(memory_space=vmem),
            pl.BlockSpec(memory_space=pl.ANY),
        ],
        out_specs=(pl.BlockSpec(memory_space=vmem), pl.BlockSpec(memory_space=vmem)),
        scratch_shapes=[
            vmem((SNAP_LOC, CH_LOC, SAMP), bf16),
            vmem((2 * BINS, SAMP), bf16),
            vmem((CH, 128), bf16),
            vmem((16, BLOCK), bf16),
            vmem((4, 16, BLOCK), bf16),
            vmem((2 * BINS, 8, 128), f32),
            vmem((BINS, 16, 128), bf16),
            vmem((ZS, 16, 128), bf16),
            vmem((8, 64, 512), bf16),
            vmem((8, 64, 512), bf16),
            vmem((4, CH, BLOCK), bf16),
            vmem((4, CH, BLOCK), bf16),
            vmem((4, 1, BLOCK), f32),
            vmem((4, 1, BLOCK), f32),
            vmem((1, BLOCK), f32),
            vmem((BINS, 1, BLOCK), f32),
            dma, dma, dma, dma, dma, dma, dma((8,)), dma, dma, dma, dma,
        ],
        compiler_params=pltpu.CompilerParams(
            collective_id=0, has_side_effects=True, vmem_limit_bytes=32 * 1024 * 1024
        ),
    )(bins, sensor_coords, grid_coords, series)
    return bin_power, power.reshape(BLOCK)


def solution(mesh):
    return jax.shard_map(
        on_device,
        mesh=mesh,
        in_specs=(P("freq", "grid", None), P(), P(), P(None, "grid")),
        out_specs=(P("freq", "grid"), P("grid")),
        check_vma=False,
    )
```

```python
import jax
import jax.numpy as jnp
from jax import lax
from jax.experimental import pallas as pl
from jax.experimental.pallas import tpu as pltpu
from jax.sharding import PartitionSpec as P

MESH = pl.DeviceIdType.MESH

SIN_COEF = (4.442883014678955, -7.308245658874512, 3.606354236602783, -0.8461116552352905, 0.1098245158791542)
COS_COEF = (1.4142135381698608, -6.978850841522217, 5.739460468292236, -1.883557915687561, 0.3106880187988281)

XS, ZS, BINS = 4, 16, 16
CH_LOC, SNAP_LOC, SAMP, BLOCK = 32, 32, 256, 256
CH = 1024
NEAR = (0, 1, 15, 2, 14, 3, 13, 4, 12, 5, 11, 6, 10, 7, 9, 8)
STEPS = (0, 3, 1, 2)


def horner(coef, z):
    acc = coef[-1] * z + coef[-2]
    for value in coef[-3::-1]:
        acc = acc * z + value
    return acc


def sincos_turns(turns):
    r = turns - jnp.round(turns)
    z = r * r
    s = horner(SIN_COEF, z) * r
    c = horner(COS_COEF, z)
    return 1.0 - s * s, s * c


def lattice(coords, flip):
    c = coords.astype(jnp.float32)
    norm = jnp.sum(c * c, axis=0, keepdims=True)
    high = jnp.floor(norm * (1.0 / 128.0)) * 128.0
    low = norm - high
    one = jnp.ones_like(norm)
    tail = (high, low, one, one) if flip else (one, one, high, low)
    scale = 1.0 if flip else -2.0
    zeros = jnp.zeros((9, c.shape[1]), jnp.float32)
    return jnp.concatenate([c * scale, *tail, zeros], axis=0)


def kernel(
    bins_hbm, sensor_hbm, grid_hbm, series_hbm, bin_power_ref, power_ref,
    bins_ref, sensor_ref, grid_ref, series_v, table_v, sensors_t, sensors_z, points_own, points, spec_f32,
    send1, recv1, slots, turned, wave_c, wave_s, sums, part, recv_a, out_b, recv_b,
    bins_sem, sensor_sem, grid_sem, series_sem, points_send, points_recv, send1_sem, recv1_sem, send2_sem, recv2_sem,
    send_a, sem_a, send_b, sem_b,
):
    f = lax.axis_index("freq")
    g = lax.axis_index("grid")
    core, x, y_hi = lax.rem(f, 2), lax.rem(f // 2, XS), f // (2 * XS)
    x_hi, x_lo = x // 2, lax.rem(x, 2)
    z, y_lo = lax.rem(g, ZS), g // ZS
    pos = x_lo * 2 + core
    own8 = pos * 2 + y_lo
    share = x_hi * 2 + y_hi
    ahead = lax.rem(pos + ZS - z, 4)
    home = ahead == 0

    def group_member(k):
        other = lax.rem(own8 + k, 8)
        lo, place = lax.rem(other, 2), other // 2
        xo = x_hi * 2 + place // 2
        return lo, place, ((y_hi * XS + xo) * 2 + lax.rem(place, 2), lo * ZS + z)

    def z_partner(k):
        zo = lax.rem(z + k, ZS)
        return zo, (f, y_lo * ZS + zo)

    loads = [
        pltpu.make_async_copy(*pair)
        for pair in (
            (bins_hbm, bins_ref, bins_sem),
            (series_hbm, series_v, series_sem),
            (grid_hbm, grid_ref, grid_sem),
            (sensor_hbm, sensor_ref, sensor_sem),
        )
    ]
    for load in loads:
        load.start()

    barrier = pltpu.get_barrier_semaphore()
    for k in NEAR[:0:-1]:
        pl.semaphore_signal(barrier, inc=1, device_id=z_partner(k)[1], device_id_type=MESH)
    for k in range(1, 4):
        other = lax.rem(share + k, 4)
        for place in range(4):
            fo = (lax.rem(other, 2) * XS + (other // 2) * 2 + place // 2) * 2 + place % 2
            pl.semaphore_signal(barrier, inc=1, device_id=(fo, g), device_id_type=MESH)
    for k in range(1, 8):
        pl.semaphore_signal(barrier, inc=1, device_id=group_member(k)[2], device_id_type=MESH)

    loads[0].wait()
    row = lax.broadcasted_iota(jnp.int32, (2 * BINS, SAMP), 0)
    time = lax.broadcasted_iota(jnp.int32, (2 * BINS, SAMP), 1)
    number = jnp.zeros((2 * BINS, SAMP), jnp.int32)
    for b in range(BINS):
        number = jnp.where(row // 2 == b, bins_ref[b], number)
    cycles = (number * time + (row % 2) * (SAMP // 4)) & (SAMP - 1)
    table_v[...] = (sincos_turns(cycles.astype(jnp.float32) * (1.0 / SAMP))[0] * (SAMP / 2.0) ** -0.5).astype(
        jnp.bfloat16
    )

    loads[1].wait()
    spec = lax.dot_general(
        table_v[...], series_v[...].reshape(SNAP_LOC * CH_LOC, SAMP),
        (((1,), (1,)), ((), ())), preferred_element_type=jnp.float32,
    )
    for t in range(8):
        spec_f32[:, t, :] = spec[:, t * 128:(t + 1) * 128]
    send1[...] = spec_f32[...].reshape(BINS, 16, 128).astype(jnp.bfloat16)

    loads[2].wait()
    points_own[...] = lattice(grid_ref[...], False).astype(jnp.bfloat16)

    loads[3].wait()
    sensors_t[...] = jnp.transpose(
        jnp.concatenate([lattice(sensor_ref[...], True), jnp.zeros((112, CH), jnp.float32)], axis=0)
    ).astype(jnp.bfloat16)
    for p in range(ZS):
        for lo in range(2):
            start = pl.multiple_of((lo * ZS + lax.rem(z + NEAR[p], ZS)) * CH_LOC, CH_LOC)
            to = (2 * (p // 4) + lo) * 128 + (p % 4) * CH_LOC
            sensors_z[to:to + CH_LOC, :] = sensors_t[pl.ds(start, CH_LOC), :]
    rate = bins_ref[z].astype(jnp.float32) * (1.0 / 128.0)

    pl.semaphore_wait(barrier, ZS - 1 + 12 + 7)

    @pl.when(home)
    def _():
        for k in NEAR[:0:-1]:
            slot = STEPS.index((ZS - k) // 4)
            pltpu.make_async_remote_copy(
                points_own, points.at[slot], points_send, points_recv.at[slot],
                device_id=z_partner(k)[1], device_id_type=MESH,
            ).start()
        pltpu.make_async_copy(points_own, points.at[0], points_recv.at[0]).start()

    for k in NEAR[:0:-1]:
        zo, device = z_partner(k)
        place = NEAR.index(ZS - k)
        pltpu.make_async_remote_copy(
            send1.at[zo], recv1.at[place], send1_sem, recv1_sem.at[place // 4], device_id=device, device_id_type=MESH
        ).start()
    pltpu.make_async_copy(send1.at[z], recv1.at[0], recv1_sem.at[0]).start()

    def replicas(i):
        pltpu.make_async_copy(points.at[i], points.at[i], points_recv.at[i]).wait()
        rhs = points[i]

        def body(n, carry):
            rows = pl.ds(pl.multiple_of(n * 128, 128), 128)
            squared = jnp.dot(sensors_z[rows, :16], rhs, preferred_element_type=jnp.float32)
            root = lax.rsqrt(jnp.maximum(squared, 0.5))
            c, s = sincos_turns((squared * rate) * root)
            wave_c[i, rows, :] = c.astype(jnp.bfloat16)
            wave_s[i, rows, :] = s.astype(jnp.bfloat16)
            return carry

        lax.fori_loop(0, CH // 128, body, 0)

    lane = lax.broadcasted_iota(jnp.int32, (16, 128), 1) // 32

    def regroup(q):
        four = recv1.at[4 * q:4 * q + 4]
        pltpu.make_async_copy(four, four, recv1_sem.at[q]).wait()
        pieces = [recv1[4 * q + j].astype(jnp.float32) for j in range(4)]
        tiles = []
        for h in range(4):
            tile = None
            for j in range(4):
                shift = ((j - h) * 32) % 128
                moved = pieces[j] if shift == 0 else pltpu.roll(pieces[j], shift, 1)
                tile = moved if tile is None else jnp.where(lane == j, moved, tile)
            tiles.append(tile)
        stacked = jnp.concatenate([t[:8] for t in tiles] + [t[8:] for t in tiles], axis=0)
        mine = pl.ds(pl.multiple_of(pos * 64, 64), 64)
        slots[q, y_lo, mine, :] = stacked.astype(jnp.bfloat16)
        block = slots.at[q, y_lo, mine]
        for k in range(1, 8):
            pltpu.make_async_remote_copy(
                block, block, send2_sem, recv2_sem.at[q, own8],
                device_id=group_member(k)[2], device_id_type=MESH,
            ).start()

    def collect(q):
        for k in range(1, 8):
            lo, place, _ = group_member(k)
            block = slots.at[q, lo, pl.ds(pl.multiple_of(place * 64, 64), 64)]
            pltpu.make_async_copy(block, block, recv2_sem.at[q, lax.rem(own8 + k, 8)]).wait()
        for lo in range(2):
            for p in range(4):
                turned[q, lo, p * 64:p * 64 + 32] = -slots[q, lo, p * 64 + 32:p * 64 + 64]
                turned[q, lo, p * 64 + 32:p * 64 + 64] = slots[q, lo, p * 64:p * 64 + 32]

    def product(i, q):
        rows = slice(q * 256, q * 256 + 256)
        direct = jnp.concatenate([slots[q, 0], slots[q, 1]], axis=1)
        crossed = jnp.concatenate([turned[q, 0], turned[q, 1]], axis=1)
        return jnp.dot(direct, wave_c[i, rows, :], preferred_element_type=jnp.float32) + jnp.dot(
            crossed, wave_s[i, rows, :], preferred_element_type=jnp.float32
        )

    replicas(0)
    regroup(0)
    regroup(1)
    replicas(1)
    regroup(2)
    replicas(2)
    regroup(3)
    replicas(3)
    for q in range(3):
        collect(q)
    for i in range(4):
        sums[i] = (product(i, 0) + product(i, 1)) + product(i, 2)
    collect(3)

    for i in range(4):
        beam = sums[i] + product(i, 3)
        part[i] = jnp.sum(beam * beam, axis=0, keepdims=True) * (1.0 / (512.0 * 1024.0))

        def send():
            target = z_partner(ahead + 4 * STEPS[i])[1]
            pltpu.make_async_remote_copy(
                part.at[i], recv_a.at[z], send_a, sem_a, device_id=target, device_id_type=MESH
            ).start()

        if i > 0:
            send()
        else:
            pl.when(jnp.logical_not(home))(send)

            @pl.when(home)
            def _():
                pltpu.make_async_copy(part.at[0], recv_a.at[z], sem_a).start()

    @pl.when(home)
    def _():
        pltpu.make_async_copy(recv_a, recv_a, sem_a).wait()
        total = recv_a[0]
        for b in range(1, BINS):
            total = total + recv_a[b]
        for b in range(BINS):
            out_b[b, :, :BLOCK] = recv_a[b]
            out_b[b, :, BLOCK:] = total
        for k in range(1, BINS):
            fo = lax.rem(f + k, BINS)
            pltpu.make_async_remote_copy(
                out_b.at[fo], recv_b.at[share], send_b, sem_b, device_id=(fo, g), device_id_type=MESH
            ).start()
        pltpu.make_async_copy(out_b.at[f], recv_b.at[share], sem_b).start()

    pltpu.make_async_copy(recv_b, recv_b, sem_b).wait()
    both = (recv_b[0] + recv_b[1]) + (recv_b[2] + recv_b[3])
    bin_power_ref[...] = both[:, :BLOCK]
    power_ref[...] = both[:, BLOCK:] * (1.0 / BINS)

    @pl.when(home)
    def _():
        sent = wave_c.at[0, 0:15 * 16]
        pltpu.make_async_copy(sent, sent, points_send).wait()
        pltpu.make_async_copy(out_b.at[0:15], out_b.at[0:15], send_b).wait()
        pltpu.make_async_copy(part.at[0:3], part.at[0:3], send_a).wait()

    @pl.when(jnp.logical_not(home))
    def _():
        pltpu.make_async_copy(part, part, send_a).wait()

    pltpu.make_async_copy(send1.at[0:15], send1.at[0:15], send1_sem).wait()
    sent = wave_c.at[:, 0:7 * 32]
    pltpu.make_async_copy(sent, sent, send2_sem).wait()


def on_device(series, bins, sensor_coords, grid_coords):
    vmem = pltpu.VMEM
    bf16, f32 = jnp.bfloat16, jnp.float32
    dma = pltpu.SemaphoreType.DMA
    bin_power, power = pl.pallas_call(
        kernel,
        out_shape=(jax.ShapeDtypeStruct((1, BLOCK), f32), jax.ShapeDtypeStruct((1, BLOCK), f32)),
        in_specs=[pl.BlockSpec(memory_space=pltpu.HBM)] * 4,
        out_specs=(pl.BlockSpec(memory_space=vmem), pl.BlockSpec(memory_space=vmem)),
        scratch_shapes=[
            pltpu.SMEM((BINS,), jnp.int32),
            vmem((3, CH), jnp.int32),
            vmem((3, BLOCK), jnp.int32),
            vmem((SNAP_LOC, CH_LOC, SAMP), bf16),
            vmem((2 * BINS, SAMP), bf16),
            vmem((CH, 128), bf16),
            vmem((CH, 128), bf16),
            vmem((16, BLOCK), bf16),
            vmem((4, 16, BLOCK), bf16),
            vmem((2 * BINS, 8, 128), f32),
            vmem((BINS, 16, 128), bf16),
            vmem((ZS, 16, 128), bf16),
            vmem((4, 2, 256, 128), bf16),
            vmem((4, 2, 256, 128), bf16),
            vmem((4, CH, BLOCK), bf16),
            vmem((4, CH, BLOCK), bf16),
            vmem((4, 256, BLOCK), f32),
            vmem((4, 1, BLOCK), f32),
            vmem((BINS, 1, BLOCK), f32),
            vmem((BINS, 1, 2 * BLOCK), f32),
            vmem((4, 1, 2 * BLOCK), f32),
            dma, dma, dma, dma, dma, dma((4,)), dma, dma((4,)), dma, dma((4, 8)), dma, dma, dma, dma,
        ],
        compiler_params=pltpu.CompilerParams(
            collective_id=0, has_side_effects=True, vmem_limit_bytes=56 * 1024 * 1024
        ),
    )(bins, sensor_coords, grid_coords, series)
    return bin_power, power.reshape(BLOCK)


def solution(mesh):
    return jax.shard_map(
        on_device,
        mesh=mesh,
        in_specs=(P("freq", "grid", None), P(), P(), P(None, "grid")),
        out_specs=(P("freq", "grid"), P("grid")),
        check_vma=False,
    )
```

```python
import jax
import jax.numpy as jnp
from jax import lax
from jax.experimental import pallas as pl
from jax.experimental.pallas import tpu as pltpu
from jax.sharding import PartitionSpec as P

MESH = pl.DeviceIdType.MESH

SIN_COEF = (4.442883014678955, -7.308245658874512, 3.606354236602783, -0.8461116552352905, 0.1098245158791542)
COS_COEF = (1.4142135381698608, -6.978850841522217, 5.739460468292236, -1.883557915687561, 0.3106880187988281)

XS, ZS, BINS = 4, 16, 16
CH_LOC, SNAP_LOC, SAMP, BLOCK = 32, 32, 256, 256
CH = 1024
NEAR = (0, 1, 15, 2, 14, 3, 13, 4, 12, 5, 11, 6, 10, 7, 9, 8)
STEPS = (0, 3, 1, 2)


def horner(coef, z):
    acc = coef[-1] * z + coef[-2]
    for value in coef[-3::-1]:
        acc = acc * z + value
    return acc


def sincos_turns(turns):
    r = turns - jnp.round(turns)
    z = r * r
    s = horner(SIN_COEF, z) * r
    c = horner(COS_COEF, z)
    return 1.0 - s * s, s * c


def lattice(coords, flip):
    c = coords.astype(jnp.float32)
    norm = jnp.sum(c * c, axis=0, keepdims=True)
    high = jnp.floor(norm * (1.0 / 128.0)) * 128.0
    low = norm - high
    one = jnp.ones_like(norm)
    tail = (high, low, one, one) if flip else (one, one, high, low)
    scale = 1.0 if flip else -2.0
    zeros = jnp.zeros((9, c.shape[1]), jnp.float32)
    return jnp.concatenate([c * scale, *tail, zeros], axis=0)


def kernel(
    bins_hbm, sensor_hbm, grid_hbm, series_hbm, bin_power_ref, power_ref,
    bins_ref, sensor_ref, grid_ref, series_v, table_v, sensors_t, sensors_z, points, spec_f32,
    send1, recv1, slots, turned, wave_c, wave_s, sums, part, recv_a, out_b, recv_b,
    bins_sem, sensor_sem, grid_sem, series_sem, points_send, points_recv, send1_sem, recv1_sem, send2_sem, recv2_sem,
    send_a, sem_a, send_b, sem_b,
):
    f = lax.axis_index("freq")
    g = lax.axis_index("grid")
    core, x, y_hi = lax.rem(f, 2), lax.rem(f // 2, XS), f // (2 * XS)
    x_hi, x_lo = x // 2, lax.rem(x, 2)
    z, y_lo = lax.rem(g, ZS), g // ZS
    pos = x_lo * 2 + core
    own8 = pos * 2 + y_lo
    share = x_hi * 2 + y_hi
    ahead = lax.rem((1 - core) * 2 + x_lo + ZS - z, 4)
    home = ahead == 0

    def group_member(k):
        other = lax.rem(own8 + k, 8)
        lo, place = lax.rem(other, 2), other // 2
        xo = x_hi * 2 + place // 2
        return lo, place, ((y_hi * XS + xo) * 2 + lax.rem(place, 2), lo * ZS + z)

    def z_partner(k):
        zo = lax.rem(z + k, ZS)
        return zo, (f, y_lo * ZS + zo)

    loads = [
        pltpu.make_async_copy(*pair)
        for pair in (
            (bins_hbm, bins_ref, bins_sem),
            (series_hbm, series_v, series_sem),
            (grid_hbm, grid_ref, grid_sem),
            (sensor_hbm, sensor_ref, sensor_sem),
        )
    ]
    for load in loads:
        load.start()

    barrier = pltpu.get_barrier_semaphore()
    for k in NEAR[:0:-1]:
        pl.semaphore_signal(barrier, inc=1, device_id=z_partner(k)[1], device_id_type=MESH)
    for k in range(1, 4):
        other = lax.rem(share + k, 4)
        for place in range(4):
            fo = (lax.rem(other, 2) * XS + (other // 2) * 2 + place // 2) * 2 + place % 2
            pl.semaphore_signal(barrier, inc=1, device_id=(fo, g), device_id_type=MESH)
    for k in range(1, 8):
        pl.semaphore_signal(barrier, inc=1, device_id=group_member(k)[2], device_id_type=MESH)

    loads[0].wait()
    row = lax.broadcasted_iota(jnp.int32, (2 * BINS, SAMP), 0)
    time = lax.broadcasted_iota(jnp.int32, (2 * BINS, SAMP), 1)
    number = jnp.zeros((2 * BINS, SAMP), jnp.int32)
    for b in range(BINS):
        number = jnp.where(row // 2 == b, bins_ref[b], number)
    cycles = (number * time + (row % 2) * (SAMP // 4)) & (SAMP - 1)
    table_v[...] = (sincos_turns(cycles.astype(jnp.float32) * (1.0 / SAMP))[0] * (SAMP / 2.0) ** -0.5).astype(
        jnp.bfloat16
    )

    loads[1].wait()
    spec = lax.dot_general(
        table_v[...], series_v[...].reshape(SNAP_LOC * CH_LOC, SAMP),
        (((1,), (1,)), ((), ())), preferred_element_type=jnp.float32,
    )
    for t in range(8):
        spec_f32[:, t, :] = spec[:, t * 128:(t + 1) * 128]
    send1[...] = spec_f32[...].reshape(BINS, 16, 128).astype(jnp.bfloat16)

    loads[3].wait()
    sensors_t[...] = jnp.transpose(
        jnp.concatenate([lattice(sensor_ref[...], True), jnp.zeros((112, CH), jnp.float32)], axis=0)
    ).astype(jnp.bfloat16)
    for p in range(ZS):
        for lo in range(2):
            start = pl.multiple_of((lo * ZS + lax.rem(z + NEAR[p], ZS)) * CH_LOC, CH_LOC)
            to = (2 * (p // 4) + lo) * 128 + (p % 4) * CH_LOC
            sensors_z[to:to + CH_LOC, :] = sensors_t[pl.ds(start, CH_LOC), :]
    rate = bins_ref[z].astype(jnp.float32) * (1.0 / 128.0)

    pl.semaphore_wait(barrier, ZS - 1 + 12 + 7)

    for k in NEAR[:0:-1]:
        zo, device = z_partner(k)
        place = NEAR.index(ZS - k)
        pltpu.make_async_remote_copy(
            send1.at[zo], recv1.at[place], send1_sem, recv1_sem.at[place // 4], device_id=device, device_id_type=MESH
        ).start()
    pltpu.make_async_copy(send1.at[z], recv1.at[0], recv1_sem.at[0]).start()

    @pl.when(home)
    def _():
        loads[2].wait()
        for k in NEAR[:0:-1]:
            slot = STEPS.index((ZS - k) // 4)
            pltpu.make_async_remote_copy(
                grid_ref, points.at[slot], points_send, points_recv.at[slot],
                device_id=z_partner(k)[1], device_id_type=MESH,
            ).start()
        pltpu.make_async_copy(grid_ref, points.at[0], points_recv.at[0]).start()

    @pl.when(jnp.logical_not(home))
    def _():
        loads[2].wait()

    def replicas(i):
        pltpu.make_async_copy(points.at[i], points.at[i], points_recv.at[i]).wait()
        rhs = lattice(points[i], False).astype(jnp.bfloat16)

        def body(n, carry):
            rows = pl.ds(pl.multiple_of(n * 128, 128), 128)
            squared = jnp.dot(sensors_z[rows, :16], rhs, preferred_element_type=jnp.float32)
            root = lax.rsqrt(jnp.maximum(squared, 0.5))
            c, s = sincos_turns((squared * rate) * root)
            wave_c[i, rows, :] = c.astype(jnp.bfloat16)
            wave_s[i, rows, :] = s.astype(jnp.bfloat16)
            return carry

        lax.fori_loop(0, CH // 128, body, 0)

    lane = lax.broadcasted_iota(jnp.int32, (16, 128), 1) // 32

    def regroup(q):
        four = recv1.at[4 * q:4 * q + 4]
        pltpu.make_async_copy(four, four, recv1_sem.at[q]).wait()
        pieces = [recv1[4 * q + j].astype(jnp.float32) for j in range(4)]
        tiles = []
        for h in range(4):
            tile = None
            for j in range(4):
                shift = ((j - h) * 32) % 128
                moved = pieces[j] if shift == 0 else pltpu.roll(pieces[j], shift, 1)
                tile = moved if tile is None else jnp.where(lane == j, moved, tile)
            tiles.append(tile)
        stacked = jnp.concatenate([t[:8] for t in tiles] + [t[8:] for t in tiles], axis=0)
        mine = pl.ds(pl.multiple_of(pos * 64, 64), 64)
        slots[q, y_lo, mine, :] = stacked.astype(jnp.bfloat16)
        block = slots.at[q, y_lo, mine]
        for k in range(1, 8):
            pltpu.make_async_remote_copy(
                block, block, send2_sem, recv2_sem.at[q, own8],
                device_id=group_member(k)[2], device_id_type=MESH,
            ).start()

    def collect(q):
        for k in range(1, 8):
            lo, place, _ = group_member(k)
            block = slots.at[q, lo, pl.ds(pl.multiple_of(place * 64, 64), 64)]
            pltpu.make_async_copy(block, block, recv2_sem.at[q, lax.rem(own8 + k, 8)]).wait()
        for lo in range(2):
            for p in range(4):
                turned[q, lo, p * 64:p * 64 + 32] = -slots[q, lo, p * 64 + 32:p * 64 + 64]
                turned[q, lo, p * 64 + 32:p * 64 + 64] = slots[q, lo, p * 64:p * 64 + 32]

    def product(i, q):
        rows = slice(q * 256, q * 256 + 256)
        direct = jnp.concatenate([slots[q, 0], slots[q, 1]], axis=1)
        crossed = jnp.concatenate([turned[q, 0], turned[q, 1]], axis=1)
        return jnp.dot(direct, wave_c[i, rows, :], preferred_element_type=jnp.float32) + jnp.dot(
            crossed, wave_s[i, rows, :], preferred_element_type=jnp.float32
        )

    replicas(0)
    regroup(0)
    regroup(1)
    replicas(1)
    regroup(2)
    replicas(2)
    regroup(3)
    replicas(3)
    for q in range(3):
        collect(q)
    for i in range(4):
        sums[i] = (product(i, 0) + product(i, 1)) + product(i, 2)
    collect(3)

    for i in range(4):
        beam = sums[i] + product(i, 3)
        part[i] = jnp.sum(beam * beam, axis=0, keepdims=True) * (1.0 / (512.0 * 1024.0))

        def send():
            target = z_partner(ahead + 4 * STEPS[i])[1]
            pltpu.make_async_remote_copy(
                part.at[i], recv_a.at[z], send_a, sem_a, device_id=target, device_id_type=MESH
            ).start()

        if i > 0:
            send()
        else:
            pl.when(jnp.logical_not(home))(send)

            @pl.when(home)
            def _():
                pltpu.make_async_copy(part.at[0], recv_a.at[z], sem_a).start()

    @pl.when(home)
    def _():
        pltpu.make_async_copy(recv_a, recv_a, sem_a).wait()
        total = recv_a[0]
        for b in range(1, BINS):
            total = total + recv_a[b]
        for b in range(BINS):
            out_b[b, :, :BLOCK] = recv_a[b]
            out_b[b, :, BLOCK:] = total
        for k in range(1, BINS):
            fo = lax.rem(f + k, BINS)
            pltpu.make_async_remote_copy(
                out_b.at[fo], recv_b.at[share], send_b, sem_b, device_id=(fo, g), device_id_type=MESH
            ).start()
        pltpu.make_async_copy(out_b.at[f], recv_b.at[share], sem_b).start()

    pltpu.make_async_copy(recv_b, recv_b, sem_b).wait()
    both = (recv_b[0] + recv_b[1]) + (recv_b[2] + recv_b[3])
    bin_power_ref[...] = both[:, :BLOCK]
    power_ref[...] = both[:, BLOCK:] * (1.0 / BINS)

    @pl.when(home)
    def _():
        for _ in range(3):
            pltpu.make_async_copy(points, points, points_send).wait()
        pltpu.make_async_copy(points.at[0:3], points.at[0:3], points_send).wait()
        pltpu.make_async_copy(out_b.at[0:15], out_b.at[0:15], send_b).wait()
        pltpu.make_async_copy(part.at[0:3], part.at[0:3], send_a).wait()

    @pl.when(jnp.logical_not(home))
    def _():
        pltpu.make_async_copy(part, part, send_a).wait()

    pltpu.make_async_copy(send1.at[0:15], send1.at[0:15], send1_sem).wait()
    sent = wave_c.at[:, 0:7 * 32]
    pltpu.make_async_copy(sent, sent, send2_sem).wait()


def on_device(series, bins, sensor_coords, grid_coords):
    vmem = pltpu.VMEM
    bf16, f32 = jnp.bfloat16, jnp.float32
    dma = pltpu.SemaphoreType.DMA
    bin_power, power = pl.pallas_call(
        kernel,
        out_shape=(jax.ShapeDtypeStruct((1, BLOCK), f32), jax.ShapeDtypeStruct((1, BLOCK), f32)),
        in_specs=[pl.BlockSpec(memory_space=pltpu.HBM)] * 4,
        out_specs=(pl.BlockSpec(memory_space=vmem), pl.BlockSpec(memory_space=vmem)),
        scratch_shapes=[
            pltpu.SMEM((BINS,), jnp.int32),
            vmem((3, CH), jnp.int32),
            vmem((3, BLOCK), jnp.int32),
            vmem((SNAP_LOC, CH_LOC, SAMP), bf16),
            vmem((2 * BINS, SAMP), bf16),
            vmem((CH, 128), bf16),
            vmem((CH, 128), bf16),
            vmem((4, 3, BLOCK), jnp.int32),
            vmem((2 * BINS, 8, 128), f32),
            vmem((BINS, 16, 128), bf16),
            vmem((ZS, 16, 128), bf16),
            vmem((4, 2, 256, 128), bf16),
            vmem((4, 2, 256, 128), bf16),
            vmem((4, CH, BLOCK), bf16),
            vmem((4, CH, BLOCK), bf16),
            vmem((4, 256, BLOCK), f32),
            vmem((4, 1, BLOCK), f32),
            vmem((BINS, 1, BLOCK), f32),
            vmem((BINS, 1, 2 * BLOCK), f32),
            vmem((4, 1, 2 * BLOCK), f32),
            dma, dma, dma, dma, dma, dma((4,)), dma, dma((4,)), dma, dma((4, 8)), dma, dma, dma, dma,
        ],
        compiler_params=pltpu.CompilerParams(
            collective_id=0, has_side_effects=True, vmem_limit_bytes=56 * 1024 * 1024
        ),
    )(bins, sensor_coords, grid_coords, series)
    return bin_power, power.reshape(BLOCK)


def solution(mesh):
    return jax.shard_map(
        on_device,
        mesh=mesh,
        in_specs=(P("freq", "grid", None), P(), P(), P(None, "grid")),
        out_specs=(P("freq", "grid"), P("grid")),
        check_vma=False,
    )
```

```python
import jax
import jax.numpy as jnp
from jax import lax
from jax.experimental import pallas as pl
from jax.experimental.pallas import tpu as pltpu
from jax.sharding import PartitionSpec as P

MESH = pl.DeviceIdType.MESH

SIN_COEF = (4.442883014678955, -7.308245658874512, 3.606354236602783, -0.8461116552352905, 0.1098245158791542)
COS_COEF = (1.4142135381698608, -6.978850841522217, 5.739460468292236, -1.883557915687561, 0.3106880187988281)

XS, ZS, BINS = 4, 16, 16
CH_LOC, SNAP_LOC, SAMP, BLOCK = 32, 32, 256, 256
CH = 1024
NEAR = (0, 1, 15, 2, 14, 3, 13, 4, 12, 5, 11, 6, 10, 7, 9, 8)
STEPS = (0, 3, 1, 2)


def horner(coef, z):
    acc = coef[-1] * z + coef[-2]
    for value in coef[-3::-1]:
        acc = acc * z + value
    return acc


def sincos_turns(turns):
    r = turns - jnp.round(turns)
    z = r * r
    s = horner(SIN_COEF, z) * r
    c = horner(COS_COEF, z)
    return 1.0 - s * s, s * c


def lattice(coords, flip):
    c = coords.astype(jnp.float32)
    norm = jnp.sum(c * c, axis=0, keepdims=True)
    high = jnp.floor(norm * (1.0 / 128.0)) * 128.0
    low = norm - high
    one = jnp.ones_like(norm)
    tail = (high, low, one, one) if flip else (one, one, high, low)
    scale = 1.0 if flip else -2.0
    zeros = jnp.zeros((9, c.shape[1]), jnp.float32)
    return jnp.concatenate([c * scale, *tail, zeros], axis=0)


def kernel(
    bins_hbm, sensor_hbm, grid_hbm, series_hbm, out_ref,
    bins_ref, sensor_ref, grid_ref, series_v, table_v, sensors_t, sensors_z, points, spec_f32,
    send1, recv1, slots, turned, wave_c, wave_s, sums, part, recv_a, out_b, recv_b,
    bins_sem, sensor_sem, grid_sem, series_sem, points_send, points_recv, send1_sem, recv1_sem, send2_sem, recv2_sem,
    send_a, sem_a, send_b, sem_b,
):
    f = lax.axis_index("freq")
    g = lax.axis_index("grid")
    core, x, y_hi = lax.rem(f, 2), lax.rem(f // 2, XS), f // (2 * XS)
    x_hi, x_lo = x // 2, lax.rem(x, 2)
    z, y_lo = lax.rem(g, ZS), g // ZS
    pos = x_lo * 2 + core
    own8 = pos * 2 + y_lo
    share = x_hi * 2 + y_hi
    ahead = lax.rem((1 - core) * 2 + x_lo + ZS - z, 4)
    home = ahead == 0

    def group_member(k):
        other = lax.rem(own8 + k, 8)
        lo, place = lax.rem(other, 2), other // 2
        xo = x_hi * 2 + place // 2
        return lo, place, ((y_hi * XS + xo) * 2 + lax.rem(place, 2), lo * ZS + z)

    def z_partner(k):
        zo = lax.rem(z + k, ZS)
        return zo, (f, y_lo * ZS + zo)

    loads = [
        pltpu.make_async_copy(*pair)
        for pair in (
            (bins_hbm, bins_ref, bins_sem),
            (series_hbm, series_v, series_sem),
            (grid_hbm, grid_ref, grid_sem),
            (sensor_hbm, sensor_ref, sensor_sem),
        )
    ]
    for load in loads:
        load.start()

    barrier = pltpu.get_barrier_semaphore()
    for k in NEAR[:0:-1]:
        pl.semaphore_signal(barrier, inc=1, device_id=z_partner(k)[1], device_id_type=MESH)
    for k in range(1, 4):
        other = lax.rem(share + k, 4)
        for place in range(4):
            fo = (lax.rem(other, 2) * XS + (other // 2) * 2 + place // 2) * 2 + place % 2
            pl.semaphore_signal(barrier, inc=1, device_id=(fo, g), device_id_type=MESH)
    for k in range(1, 8):
        pl.semaphore_signal(barrier, inc=1, device_id=group_member(k)[2], device_id_type=MESH)

    loads[0].wait()
    row = lax.broadcasted_iota(jnp.int32, (2 * BINS, SAMP), 0)
    time = lax.broadcasted_iota(jnp.int32, (2 * BINS, SAMP), 1)
    number = jnp.zeros((2 * BINS, SAMP), jnp.int32)
    for b in range(BINS):
        number = jnp.where(row // 2 == b, bins_ref[b], number)
    cycles = (number * time + (row % 2) * (SAMP // 4)) & (SAMP - 1)
    table_v[...] = (sincos_turns(cycles.astype(jnp.float32) * (1.0 / SAMP))[0] * (SAMP / 2.0) ** -0.5).astype(
        jnp.bfloat16
    )

    loads[1].wait()
    spec = lax.dot_general(
        table_v[...], series_v[...].reshape(SNAP_LOC * CH_LOC, SAMP),
        (((1,), (1,)), ((), ())), preferred_element_type=jnp.float32,
    )
    for t in range(8):
        spec_f32[:, t, :] = spec[:, t * 128:(t + 1) * 128]
    send1[...] = spec_f32[...].reshape(BINS, 16, 128).astype(jnp.bfloat16)

    loads[3].wait()
    sensors_t[...] = jnp.transpose(
        jnp.concatenate([lattice(sensor_ref[...], True), jnp.zeros((112, CH), jnp.float32)], axis=0)
    ).astype(jnp.bfloat16)
    for p in range(ZS):
        for lo in range(2):
            start = pl.multiple_of((lo * ZS + lax.rem(z + NEAR[p], ZS)) * CH_LOC, CH_LOC)
            to = (2 * (p // 4) + lo) * 128 + (p % 4) * CH_LOC
            sensors_z[to:to + CH_LOC, :] = sensors_t[pl.ds(start, CH_LOC), :]
    rate = bins_ref[z].astype(jnp.float32) * (1.0 / 128.0)

    pl.semaphore_wait(barrier, ZS - 1 + 12 + 7)

    for k in NEAR[:0:-1]:
        zo, device = z_partner(k)
        place = NEAR.index(ZS - k)
        pltpu.make_async_remote_copy(
            send1.at[zo], recv1.at[place], send1_sem, recv1_sem.at[place // 4], device_id=device, device_id_type=MESH
        ).start()
    pltpu.make_async_copy(send1.at[z], recv1.at[0], recv1_sem.at[0]).start()

    @pl.when(home)
    def _():
        loads[2].wait()
        for k in NEAR[:0:-1]:
            slot = STEPS.index((ZS - k) // 4)
            pltpu.make_async_remote_copy(
                grid_ref, points.at[slot], points_send, points_recv.at[slot],
                device_id=z_partner(k)[1], device_id_type=MESH,
            ).start()
        pltpu.make_async_copy(grid_ref, points.at[0], points_recv.at[0]).start()

    @pl.when(jnp.logical_not(home))
    def _():
        loads[2].wait()

    def replicas(i):
        pltpu.make_async_copy(points.at[i], points.at[i], points_recv.at[i]).wait()
        rhs = lattice(points[i], False).astype(jnp.bfloat16)

        def body(n, carry):
            rows = pl.ds(pl.multiple_of(n * 128, 128), 128)
            squared = jnp.dot(sensors_z[rows, :16], rhs, preferred_element_type=jnp.float32)
            root = lax.rsqrt(jnp.maximum(squared, 0.5))
            c, s = sincos_turns((squared * rate) * root)
            wave_c[i, rows, :] = c.astype(jnp.bfloat16)
            wave_s[i, rows, :] = s.astype(jnp.bfloat16)
            return carry

        lax.fori_loop(0, CH // 128, body, 0)

    lane = lax.broadcasted_iota(jnp.int32, (16, 128), 1) // 32

    def regroup(q):
        four = recv1.at[4 * q:4 * q + 4]
        pltpu.make_async_copy(four, four, recv1_sem.at[q]).wait()
        pieces = [recv1[4 * q + j].astype(jnp.float32) for j in range(4)]
        tiles = []
        for h in range(4):
            tile = None
            for j in range(4):
                shift = ((j - h) * 32) % 128
                moved = pieces[j] if shift == 0 else pltpu.roll(pieces[j], shift, 1)
                tile = moved if tile is None else jnp.where(lane == j, moved, tile)
            tiles.append(tile)
        stacked = jnp.concatenate([t[:8] for t in tiles] + [t[8:] for t in tiles], axis=0)
        mine = pl.ds(pl.multiple_of(pos * 64, 64), 64)
        slots[q, y_lo, mine, :] = stacked.astype(jnp.bfloat16)
        block = slots.at[q, y_lo, mine]
        for k in range(1, 8):
            pltpu.make_async_remote_copy(
                block, block, send2_sem, recv2_sem.at[q, own8],
                device_id=group_member(k)[2], device_id_type=MESH,
            ).start()

    def collect(q):
        for k in range(1, 8):
            lo, place, _ = group_member(k)
            block = slots.at[q, lo, pl.ds(pl.multiple_of(place * 64, 64), 64)]
            pltpu.make_async_copy(block, block, recv2_sem.at[q, lax.rem(own8 + k, 8)]).wait()
        for lo in range(2):
            for p in range(4):
                turned[q, lo, p * 64:p * 64 + 32] = -slots[q, lo, p * 64 + 32:p * 64 + 64]
                turned[q, lo, p * 64 + 32:p * 64 + 64] = slots[q, lo, p * 64:p * 64 + 32]

    def product(i, q):
        rows = slice(q * 256, q * 256 + 256)
        direct = jnp.concatenate([slots[q, 0], slots[q, 1]], axis=1)
        crossed = jnp.concatenate([turned[q, 0], turned[q, 1]], axis=1)
        return jnp.dot(direct, wave_c[i, rows, :], preferred_element_type=jnp.float32) + jnp.dot(
            crossed, wave_s[i, rows, :], preferred_element_type=jnp.float32
        )

    replicas(0)
    regroup(0)
    regroup(1)
    replicas(1)
    regroup(2)
    replicas(2)
    regroup(3)
    replicas(3)
    collect(0)
    collect(1)
    for i in range(4):
        sums[i] = product(i, 0) + product(i, 1)
    collect(2)
    for i in range(4):
        sums[i] += product(i, 2)
    collect(3)

    for i in range(4):
        beam = sums[i] + product(i, 3)
        part[i] = jnp.sum(beam * beam, axis=0, keepdims=True) * (1.0 / (512.0 * 1024.0))

        def send():
            target = z_partner(ahead + 4 * STEPS[i])[1]
            pltpu.make_async_remote_copy(
                part.at[i], recv_a.at[z], send_a, sem_a, device_id=target, device_id_type=MESH
            ).start()

        if i > 0:
            send()
        else:
            pl.when(jnp.logical_not(home))(send)

            @pl.when(home)
            def _():
                pltpu.make_async_copy(part.at[0], recv_a.at[z], sem_a).start()

    @pl.when(home)
    def _():
        pltpu.make_async_copy(recv_a, recv_a, sem_a).wait()
        total = recv_a[0]
        for b in range(1, BINS):
            total = total + recv_a[b]
        for b in range(BINS):
            out_b[b, :, :BLOCK] = recv_a[b]
            out_b[b, :, BLOCK:] = total
        for k in range(1, BINS):
            fo = lax.rem(f + k, BINS)
            pltpu.make_async_remote_copy(
                out_b.at[fo], recv_b.at[share], send_b, sem_b, device_id=(fo, g), device_id_type=MESH
            ).start()
        pltpu.make_async_copy(out_b.at[f], recv_b.at[share], sem_b).start()

    pltpu.make_async_copy(recv_b, recv_b, sem_b).wait()
    both = (recv_b[0] + recv_b[1]) + (recv_b[2] + recv_b[3])
    out_ref[...] = both

    @pl.when(home)
    def _():
        for _ in range(3):
            pltpu.make_async_copy(points, points, points_send).wait()
        pltpu.make_async_copy(points.at[0:3], points.at[0:3], points_send).wait()
        pltpu.make_async_copy(out_b.at[0:15], out_b.at[0:15], send_b).wait()
        pltpu.make_async_copy(part.at[0:3], part.at[0:3], send_a).wait()

    @pl.when(jnp.logical_not(home))
    def _():
        pltpu.make_async_copy(part, part, send_a).wait()

    pltpu.make_async_copy(send1.at[0:15], send1.at[0:15], send1_sem).wait()
    sent = wave_c.at[:, 0:7 * 32]
    pltpu.make_async_copy(sent, sent, send2_sem).wait()


def on_device(series, bins, sensor_coords, grid_coords):
    vmem = pltpu.VMEM
    bf16, f32 = jnp.bfloat16, jnp.float32
    dma = pltpu.SemaphoreType.DMA
    both = pl.pallas_call(
        kernel,
        out_shape=vmem((1, 2 * BLOCK), f32),
        in_specs=[pl.BlockSpec(memory_space=pltpu.HBM)] * 4,
        out_specs=pl.BlockSpec(memory_space=vmem),
        scratch_shapes=[
            pltpu.SMEM((BINS,), jnp.int32),
            vmem((3, CH), jnp.int32),
            vmem((3, BLOCK), jnp.int32),
            vmem((SNAP_LOC, CH_LOC, SAMP), bf16),
            vmem((2 * BINS, SAMP), bf16),
            vmem((CH, 128), bf16),
            vmem((CH, 128), bf16),
            vmem((4, 3, BLOCK), jnp.int32),
            vmem((2 * BINS, 8, 128), f32),
            vmem((BINS, 16, 128), bf16),
            vmem((ZS, 16, 128), bf16),
            vmem((4, 2, 256, 128), bf16),
            vmem((4, 2, 256, 128), bf16),
            vmem((4, CH, BLOCK), bf16),
            vmem((4, CH, BLOCK), bf16),
            vmem((4, 256, BLOCK), f32),
            vmem((4, 1, BLOCK), f32),
            vmem((BINS, 1, BLOCK), f32),
            vmem((BINS, 1, 2 * BLOCK), f32),
            vmem((4, 1, 2 * BLOCK), f32),
            dma, dma, dma, dma, dma, dma((4,)), dma, dma((4,)), dma, dma((4, 8)), dma, dma, dma, dma,
        ],
        compiler_params=pltpu.CompilerParams(
            collective_id=0, has_side_effects=True, vmem_limit_bytes=56 * 1024 * 1024
        ),
    )(bins, sensor_coords, grid_coords, series)
    return both[:, :BLOCK], both[0, BLOCK:] * (1.0 / BINS)


def solution(mesh):
    return jax.shard_map(
        on_device,
        mesh=mesh,
        in_specs=(P("freq", "grid", None), P(), P(), P(None, "grid")),
        out_specs=(P("freq", "grid"), P("grid")),
        check_vma=False,
    )
```

```python
import jax
import jax.numpy as jnp
from jax import lax
from jax.experimental import pallas as pl
from jax.experimental.pallas import tpu as pltpu
from jax.sharding import PartitionSpec as P

MESH = pl.DeviceIdType.MESH

SIN_COEF = (4.442883014678955, -7.308245658874512, 3.606354236602783, -0.8461116552352905, 0.1098245158791542)
COS_COEF = (1.4142135381698608, -6.978850841522217, 5.739460468292236, -1.883557915687561, 0.3106880187988281)

XS, ZS, BINS = 4, 16, 16
CH_LOC, SNAP_LOC, SAMP, BLOCK = 32, 32, 256, 256
CH = 1024
NEAR = (0, 1, 15, 2, 14, 3, 13, 4, 12, 5, 11, 6, 10, 7, 9, 8)
STEPS = (0, 3, 1, 2)


def horner(coef, z):
    acc = coef[-1] * z + coef[-2]
    for value in coef[-3::-1]:
        acc = acc * z + value
    return acc


def sincos_turns(turns):
    r = turns - jnp.round(turns)
    z = r * r
    s = horner(SIN_COEF, z) * r
    c = horner(COS_COEF, z)
    return 1.0 - s * s, s * c


def lattice(coords, flip):
    c = coords.astype(jnp.float32)
    norm = jnp.sum(c * c, axis=0, keepdims=True)
    high = jnp.floor(norm * (1.0 / 128.0)) * 128.0
    low = norm - high
    one = jnp.ones_like(norm)
    tail = (high, low, one, one) if flip else (one, one, high, low)
    scale = 1.0 if flip else -2.0
    zeros = jnp.zeros((9, c.shape[1]), jnp.float32)
    return jnp.concatenate([c * scale, *tail, zeros], axis=0)


def kernel(
    bins_hbm, sensor_hbm, grid_hbm, series_hbm, out_ref,
    bins_ref, sensor_ref, grid_ref, series_v, table_v, sensors_t, sensors_z, points, spec_f32,
    send1, recv1, slots, turned, wave_c, wave_s, sums, part, recv_a, out_b, recv_b,
    bins_sem, sensor_sem, grid_sem, series_sem, points_send, points_recv, send1_sem, recv1_sem, send2_sem, recv2_sem,
    send_a, sem_a, send_b, sem_b,
):
    f = lax.axis_index("freq")
    g = lax.axis_index("grid")
    core, x, y_hi = lax.rem(f, 2), lax.rem(f // 2, XS), f // (2 * XS)
    x_hi, x_lo = x // 2, lax.rem(x, 2)
    z, y_lo = lax.rem(g, ZS), g // ZS
    pos = x_lo * 2 + core
    own8 = pos * 2 + y_lo
    share = x_hi * 2 + y_hi
    ahead = lax.rem((1 - core) * 2 + 1 - x_lo + ZS - z, 4)
    holds = ahead == 0
    home = jnp.logical_and(core == 1, lax.rem(z, 2) != x_lo)

    def group_member(k):
        other = lax.rem(own8 + k, 8)
        lo, place = lax.rem(other, 2), other // 2
        xo = x_hi * 2 + place // 2
        return lo, place, ((y_hi * XS + xo) * 2 + lax.rem(place, 2), lo * ZS + z)

    def z_partner(k):
        zo = lax.rem(z + k, ZS)
        return zo, (f, y_lo * ZS + zo)

    loads = [
        pltpu.make_async_copy(*pair)
        for pair in (
            (bins_hbm, bins_ref, bins_sem),
            (series_hbm, series_v, series_sem),
            (grid_hbm, grid_ref, grid_sem),
            (sensor_hbm, sensor_ref, sensor_sem),
        )
    ]
    for load in loads:
        load.start()

    barrier = pltpu.get_barrier_semaphore()
    for k in NEAR[:0:-1]:
        pl.semaphore_signal(barrier, inc=1, device_id=z_partner(k)[1], device_id_type=MESH)
    for k in range(1, 4):
        other = lax.rem(share + k, 4)
        for place in range(4):
            fo = (lax.rem(other, 2) * XS + (other // 2) * 2 + place // 2) * 2 + place % 2
            pl.semaphore_signal(barrier, inc=1, device_id=(fo, g), device_id_type=MESH)
    for k in range(1, 8):
        pl.semaphore_signal(barrier, inc=1, device_id=group_member(k)[2], device_id_type=MESH)

    loads[0].wait()
    row = lax.broadcasted_iota(jnp.int32, (2 * BINS, SAMP), 0)
    time = lax.broadcasted_iota(jnp.int32, (2 * BINS, SAMP), 1)
    number = jnp.zeros((2 * BINS, SAMP), jnp.int32)
    for b in range(BINS):
        number = jnp.where(row // 2 == b, bins_ref[b], number)
    cycles = (number * time + (row % 2) * (SAMP // 4)) & (SAMP - 1)
    table_v[...] = (sincos_turns(cycles.astype(jnp.float32) * (1.0 / SAMP))[0] * (SAMP / 2.0) ** -0.5).astype(
        jnp.bfloat16
    )

    loads[1].wait()
    spec = lax.dot_general(
        table_v[...], series_v[...].reshape(SNAP_LOC * CH_LOC, SAMP),
        (((1,), (1,)), ((), ())), preferred_element_type=jnp.float32,
    )
    for t in range(8):
        spec_f32[:, t, :] = spec[:, t * 128:(t + 1) * 128]
    send1[...] = spec_f32[...].reshape(BINS, 16, 128).astype(jnp.bfloat16)

    loads[3].wait()
    sensors_t[...] = jnp.transpose(
        jnp.concatenate([lattice(sensor_ref[...], True), jnp.zeros((112, CH), jnp.float32)], axis=0)
    ).astype(jnp.bfloat16)
    for p in range(ZS):
        for lo in range(2):
            start = pl.multiple_of((lo * ZS + lax.rem(z + NEAR[p], ZS)) * CH_LOC, CH_LOC)
            to = (2 * (p // 4) + lo) * 128 + (p % 4) * CH_LOC
            sensors_z[to:to + CH_LOC, :] = sensors_t[pl.ds(start, CH_LOC), :]
    rate = bins_ref[z].astype(jnp.float32) * (1.0 / 128.0)

    pl.semaphore_wait(barrier, ZS - 1 + 12 + 7)

    for k in NEAR[1:]:
        zo, device = z_partner(k)
        place = NEAR.index(ZS - k)
        pltpu.make_async_remote_copy(
            send1.at[zo], recv1.at[place], send1_sem, recv1_sem.at[place // 4], device_id=device, device_id_type=MESH
        ).start()
    pltpu.make_async_copy(send1.at[z], recv1.at[0], recv1_sem.at[0]).start()

    @pl.when(holds)
    def _():
        loads[2].wait()
        for k in NEAR[:0:-1]:
            slot = STEPS.index((ZS - k) // 4)
            pltpu.make_async_remote_copy(
                grid_ref, points.at[slot], points_send, points_recv.at[slot],
                device_id=z_partner(k)[1], device_id_type=MESH,
            ).start()
        pltpu.make_async_copy(grid_ref, points.at[0], points_recv.at[0]).start()

    @pl.when(jnp.logical_not(holds))
    def _():
        loads[2].wait()

    def replicas(i):
        pltpu.make_async_copy(points.at[i], points.at[i], points_recv.at[i]).wait()
        rhs = lattice(points[i], False).astype(jnp.bfloat16)

        def body(n, carry):
            rows = pl.ds(pl.multiple_of(n * 128, 128), 128)
            squared = jnp.dot(sensors_z[rows, :16], rhs, preferred_element_type=jnp.float32)
            root = lax.rsqrt(jnp.maximum(squared, 0.5))
            c, s = sincos_turns((squared * rate) * root)
            wave_c[i, rows, :] = c.astype(jnp.bfloat16)
            wave_s[i, rows, :] = s.astype(jnp.bfloat16)
            return carry

        lax.fori_loop(0, CH // 128, body, 0)

    lane = lax.broadcasted_iota(jnp.int32, (16, 128), 1) // 32

    def regroup(q):
        four = recv1.at[4 * q:4 * q + 4]
        pltpu.make_async_copy(four, four, recv1_sem.at[q]).wait()
        pieces = [recv1[4 * q + j].astype(jnp.float32) for j in range(4)]
        tiles = []
        for h in range(4):
            tile = None
            for j in range(4):
                shift = ((j - h) * 32) % 128
                moved = pieces[j] if shift == 0 else pltpu.roll(pieces[j], shift, 1)
                tile = moved if tile is None else jnp.where(lane == j, moved, tile)
            tiles.append(tile)
        stacked = jnp.concatenate([t[:8] for t in tiles] + [t[8:] for t in tiles], axis=0)
        mine = pl.ds(pl.multiple_of(pos * 64, 64), 64)
        slots[q, y_lo, mine, :] = stacked.astype(jnp.bfloat16)
        block = slots.at[q, y_lo, mine]
        for k in range(1, 8):
            pltpu.make_async_remote_copy(
                block, block, send2_sem, recv2_sem.at[q, own8],
                device_id=group_member(k)[2], device_id_type=MESH,
            ).start()

    def collect(q):
        for k in range(1, 8):
            lo, place, _ = group_member(k)
            block = slots.at[q, lo, pl.ds(pl.multiple_of(place * 64, 64), 64)]
            pltpu.make_async_copy(block, block, recv2_sem.at[q, lax.rem(own8 + k, 8)]).wait()
        for lo in range(2):
            for p in range(4):
                turned[q, lo, p * 64:p * 64 + 32] = -slots[q, lo, p * 64 + 32:p * 64 + 64]
                turned[q, lo, p * 64 + 32:p * 64 + 64] = slots[q, lo, p * 64:p * 64 + 32]

    def product(i, q):
        rows = slice(q * 256, q * 256 + 256)
        direct = jnp.concatenate([slots[q, 0], slots[q, 1]], axis=1)
        crossed = jnp.concatenate([turned[q, 0], turned[q, 1]], axis=1)
        return jnp.dot(direct, wave_c[i, rows, :], preferred_element_type=jnp.float32) + jnp.dot(
            crossed, wave_s[i, rows, :], preferred_element_type=jnp.float32
        )

    regroup(0)
    replicas(0)
    regroup(1)
    replicas(1)
    regroup(2)
    regroup(3)
    replicas(2)
    replicas(3)
    collect(0)
    collect(1)
    for i in range(4):
        sums[i] = product(i, 0) + product(i, 1)
    collect(2)
    for i in range(4):
        sums[i] += product(i, 2)
    collect(3)

    for i in range(4):
        beam = sums[i] + product(i, 3)
        part[i] = jnp.sum(beam * beam, axis=0, keepdims=True) * (1.0 / (512.0 * 1024.0))

        def send():
            target = (f + 1 - core, z_partner(ahead + 4 * STEPS[i])[1][1])
            pltpu.make_async_remote_copy(
                part.at[i], recv_a.at[z], send_a, sem_a, device_id=target, device_id_type=MESH
            ).start()

        if i > 0:
            send()
        else:
            stays = jnp.logical_and(holds, core == 1)
            pl.when(jnp.logical_not(stays))(send)

            @pl.when(stays)
            def _():
                pltpu.make_async_copy(part.at[0], recv_a.at[z], sem_a).start()

    @pl.when(home)
    def _():
        pltpu.make_async_copy(recv_a, recv_a, sem_a).wait()
        total = recv_a[0]
        for b in range(1, BINS):
            total = total + recv_a[b]
        for b in range(BINS):
            out_b[b, :, :BLOCK] = recv_a[b]
            out_b[b, :, BLOCK:] = total
        for k in range(1, BINS):
            fo = lax.rem(f + k, BINS)
            pltpu.make_async_remote_copy(
                out_b.at[fo], recv_b.at[share], send_b, sem_b, device_id=(fo, g), device_id_type=MESH
            ).start()
        pltpu.make_async_copy(out_b.at[f], recv_b.at[share], sem_b).start()

    pltpu.make_async_copy(recv_b, recv_b, sem_b).wait()
    both = (recv_b[0] + recv_b[1]) + (recv_b[2] + recv_b[3])
    out_ref[...] = both

    @pl.when(holds)
    def _():
        for _ in range(3):
            pltpu.make_async_copy(points, points, points_send).wait()
        pltpu.make_async_copy(points.at[0:3], points.at[0:3], points_send).wait()

    @pl.when(home)
    def _():
        pltpu.make_async_copy(out_b.at[0:15], out_b.at[0:15], send_b).wait()

    pltpu.make_async_copy(part.at[0:3], part.at[0:3], send_a).wait()

    @pl.when(jnp.logical_not(jnp.logical_and(holds, core == 1)))
    def _():
        pltpu.make_async_copy(part.at[0], part.at[0], send_a).wait()

    pltpu.make_async_copy(send1.at[0:15], send1.at[0:15], send1_sem).wait()
    sent = wave_c.at[:, 0:7 * 32]
    pltpu.make_async_copy(sent, sent, send2_sem).wait()


def on_device(series, bins, sensor_coords, grid_coords):
    vmem = pltpu.VMEM
    bf16, f32 = jnp.bfloat16, jnp.float32
    dma = pltpu.SemaphoreType.DMA
    both = pl.pallas_call(
        kernel,
        out_shape=vmem((1, 2 * BLOCK), f32),
        in_specs=[pl.BlockSpec(memory_space=pltpu.HBM)] * 4,
        out_specs=pl.BlockSpec(memory_space=vmem),
        scratch_shapes=[
            pltpu.SMEM((BINS,), jnp.int32),
            vmem((3, CH), jnp.int32),
            vmem((3, BLOCK), jnp.int32),
            vmem((SNAP_LOC, CH_LOC, SAMP), bf16),
            vmem((2 * BINS, SAMP), bf16),
            vmem((CH, 128), bf16),
            vmem((CH, 128), bf16),
            vmem((4, 3, BLOCK), jnp.int32),
            vmem((2 * BINS, 8, 128), f32),
            vmem((BINS, 16, 128), bf16),
            vmem((ZS, 16, 128), bf16),
            vmem((4, 2, 256, 128), bf16),
            vmem((4, 2, 256, 128), bf16),
            vmem((4, CH, BLOCK), bf16),
            vmem((4, CH, BLOCK), bf16),
            vmem((4, 256, BLOCK), f32),
            vmem((4, 1, BLOCK), f32),
            vmem((BINS, 1, BLOCK), f32),
            vmem((BINS, 1, 2 * BLOCK), f32),
            vmem((4, 1, 2 * BLOCK), f32),
            dma, dma, dma, dma, dma, dma((4,)), dma, dma((4,)), dma, dma((4, 8)), dma, dma, dma, dma,
        ],
        compiler_params=pltpu.CompilerParams(
            collective_id=0, has_side_effects=True, vmem_limit_bytes=56 * 1024 * 1024
        ),
    )(bins, sensor_coords, grid_coords, series)
    return both[:, :BLOCK], both[0, BLOCK:] * (1.0 / BINS)


def solution(mesh):
    return jax.shard_map(
        on_device,
        mesh=mesh,
        in_specs=(P("freq", "grid", None), P(), P(), P(None, "grid")),
        out_specs=(P("freq", "grid"), P("grid")),
        check_vma=False,
    )
```

```python
import jax
import jax.numpy as jnp
from jax import lax
from jax.experimental import pallas as pl
from jax.experimental.pallas import tpu as pltpu
from jax.sharding import PartitionSpec as P

MESH = pl.DeviceIdType.MESH

SIN_COEF = (4.442883014678955, -7.308245658874512, 3.606354236602783, -0.8461116552352905, 0.1098245158791542)
COS_COEF = (1.4142135381698608, -6.978850841522217, 5.739460468292236, -1.883557915687561, 0.3106880187988281)

XS, ZS, BINS = 4, 16, 16
CH_LOC, SNAP_LOC, SAMP, BLOCK = 32, 32, 256, 256
CH = 1024
NEAR = (0, 1, 15, 2, 14, 3, 13, 4, 12, 5, 11, 6, 10, 7, 9, 8)
STEPS = (0, 3, 1, 2)


def horner(coef, z):
    acc = coef[-1] * z + coef[-2]
    for value in coef[-3::-1]:
        acc = acc * z + value
    return acc


def sincos_turns(turns):
    r = turns - jnp.round(turns)
    z = r * r
    s = horner(SIN_COEF, z) * r
    c = horner(COS_COEF, z)
    return 1.0 - s * s, s * c


def lattice(coords, flip):
    c = coords.astype(jnp.float32)
    norm = jnp.sum(c * c, axis=0, keepdims=True)
    high = jnp.floor(norm * (1.0 / 128.0)) * 128.0
    low = norm - high
    one = jnp.ones_like(norm)
    tail = (high, low, one, one) if flip else (one, one, high, low)
    scale = 1.0 if flip else -2.0
    zeros = jnp.zeros((9, c.shape[1]), jnp.float32)
    return jnp.concatenate([c * scale, *tail, zeros], axis=0)


def kernel(
    bins_hbm, sensor_hbm, grid_hbm, series_hbm, out_ref,
    bins_ref, sensor_ref, grid_ref, series_v, table_v, sensors_t, sensors_z, points, spec_f32,
    send1, recv1, slots, turned, wave_c, wave_s, sums, part, recv_a, out_b, recv_b,
    bins_sem, sensor_sem, grid_sem, series_sem, points_send, points_recv, send1_sem, recv1_sem, send2_sem, recv2_sem,
    send_a, sem_a, send_b, sem_b,
):
    f = lax.axis_index("freq")
    g = lax.axis_index("grid")
    core, x, y_hi = lax.rem(f, 2), lax.rem(f // 2, XS), f // (2 * XS)
    x_hi, x_lo = x // 2, lax.rem(x, 2)
    z, y_lo = lax.rem(g, ZS), g // ZS
    pos = x_lo * 2 + core
    own8 = pos * 2 + y_lo
    share = x_hi * 2 + y_hi
    ahead = lax.rem((1 - core) * 2 + 1 - x_lo + ZS - z, 4)
    holds = ahead == 0
    home = jnp.logical_and(core == 1, lax.rem(z, 2) != x_lo)

    def group_member(k):
        other = lax.rem(own8 + k, 8)
        lo, place = lax.rem(other, 2), other // 2
        xo = x_hi * 2 + place // 2
        return lo, place, ((y_hi * XS + xo) * 2 + lax.rem(place, 2), lo * ZS + z)

    def z_partner(k):
        zo = lax.rem(z + k, ZS)
        return zo, (f, y_lo * ZS + zo)

    loads = [
        pltpu.make_async_copy(*pair)
        for pair in (
            (bins_hbm, bins_ref, bins_sem),
            (series_hbm, series_v, series_sem),
            (grid_hbm, grid_ref, grid_sem),
            (sensor_hbm, sensor_ref, sensor_sem),
        )
    ]
    for load in loads:
        load.start()

    barrier = pltpu.get_barrier_semaphore()
    for k in NEAR[:0:-1]:
        pl.semaphore_signal(barrier, inc=1, device_id=z_partner(k)[1], device_id_type=MESH)
    for k in range(1, 4):
        other = lax.rem(share + k, 4)
        for place in range(4):
            fo = (lax.rem(other, 2) * XS + (other // 2) * 2 + place // 2) * 2 + place % 2
            pl.semaphore_signal(barrier, inc=1, device_id=(fo, g), device_id_type=MESH)
    for k in range(1, 8):
        pl.semaphore_signal(barrier, inc=1, device_id=group_member(k)[2], device_id_type=MESH)

    loads[0].wait()
    row = lax.broadcasted_iota(jnp.int32, (2 * BINS, SAMP), 0)
    time = lax.broadcasted_iota(jnp.int32, (2 * BINS, SAMP), 1)
    number = jnp.zeros((2 * BINS, SAMP), jnp.int32)
    for b in range(BINS):
        number = jnp.where(row // 2 == b, bins_ref[b], number)
    cycles = (number * time + (row % 2) * (SAMP // 4)) & (SAMP - 1)
    table_v[...] = (sincos_turns(cycles.astype(jnp.float32) * (1.0 / SAMP))[0] * (SAMP / 2.0) ** -0.5).astype(
        jnp.bfloat16
    )

    loads[1].wait()
    spec = lax.dot_general(
        table_v[...], series_v[...].reshape(SNAP_LOC * CH_LOC, SAMP),
        (((1,), (1,)), ((), ())), preferred_element_type=jnp.float32,
    )
    for t in range(8):
        spec_f32[:, t, :] = spec[:, t * 128:(t + 1) * 128]
    send1[...] = spec_f32[...].reshape(BINS, 16, 128).astype(jnp.bfloat16)

    loads[3].wait()
    sensors_t[...] = jnp.transpose(
        jnp.concatenate([lattice(sensor_ref[...], True), jnp.zeros((112, CH), jnp.float32)], axis=0)
    ).astype(jnp.bfloat16)
    for p in range(ZS):
        for lo in range(2):
            start = pl.multiple_of((lo * ZS + lax.rem(z + NEAR[p], ZS)) * CH_LOC, CH_LOC)
            to = (2 * (p // 4) + lo) * 128 + (p % 4) * CH_LOC
            sensors_z[to:to + CH_LOC, :] = sensors_t[pl.ds(start, CH_LOC), :]
    rate = bins_ref[z].astype(jnp.float32) * (1.0 / 128.0)

    pl.semaphore_wait(barrier, ZS - 1 + 12 + 7)

    for k in NEAR[1:]:
        zo, device = z_partner(k)
        place = NEAR.index(ZS - k)
        pltpu.make_async_remote_copy(
            send1.at[zo], recv1.at[place], send1_sem, recv1_sem.at[place // 4], device_id=device, device_id_type=MESH
        ).start()
    pltpu.make_async_copy(send1.at[z], recv1.at[0], recv1_sem.at[0]).start()

    @pl.when(holds)
    def _():
        loads[2].wait()
        for k in NEAR[1:]:
            slot = STEPS.index((ZS - k) // 4)
            pltpu.make_async_remote_copy(
                grid_ref, points.at[slot], points_send, points_recv.at[slot],
                device_id=z_partner(k)[1], device_id_type=MESH,
            ).start()
        pltpu.make_async_copy(grid_ref, points.at[0], points_recv.at[0]).start()

    @pl.when(jnp.logical_not(holds))
    def _():
        loads[2].wait()

    def replicas(i):
        pltpu.make_async_copy(points.at[i], points.at[i], points_recv.at[i]).wait()
        rhs = lattice(points[i], False).astype(jnp.bfloat16)

        def body(n, carry):
            rows = pl.ds(pl.multiple_of(n * 128, 128), 128)
            squared = jnp.dot(sensors_z[rows, :16], rhs, preferred_element_type=jnp.float32)
            root = lax.rsqrt(jnp.maximum(squared, 0.5))
            c, s = sincos_turns((squared * rate) * root)
            wave_c[i, rows, :] = c.astype(jnp.bfloat16)
            wave_s[i, rows, :] = s.astype(jnp.bfloat16)
            return carry

        lax.fori_loop(0, CH // 128, body, 0)

    lane = lax.broadcasted_iota(jnp.int32, (16, 128), 1) // 32

    def regroup(q):
        four = recv1.at[4 * q:4 * q + 4]
        pltpu.make_async_copy(four, four, recv1_sem.at[q]).wait()
        pieces = [recv1[4 * q + j].astype(jnp.float32) for j in range(4)]
        tiles = []
        for h in range(4):
            tile = None
            for j in range(4):
                shift = ((j - h) * 32) % 128
                moved = pieces[j] if shift == 0 else pltpu.roll(pieces[j], shift, 1)
                tile = moved if tile is None else jnp.where(lane == j, moved, tile)
            tiles.append(tile)
        stacked = jnp.concatenate([t[:8] for t in tiles] + [t[8:] for t in tiles], axis=0)
        mine = pl.ds(pl.multiple_of(pos * 64, 64), 64)
        slots[q, y_lo, mine, :] = stacked.astype(jnp.bfloat16)
        block = slots.at[q, y_lo, mine]
        for k in range(1, 8):
            pltpu.make_async_remote_copy(
                block, block, send2_sem, recv2_sem.at[q, own8],
                device_id=group_member(k)[2], device_id_type=MESH,
            ).start()

    def collect(q):
        for k in range(1, 8):
            lo, place, _ = group_member(k)
            block = slots.at[q, lo, pl.ds(pl.multiple_of(place * 64, 64), 64)]
            pltpu.make_async_copy(block, block, recv2_sem.at[q, lax.rem(own8 + k, 8)]).wait()
        for lo in range(2):
            for p in range(4):
                turned[q, lo, p * 64:p * 64 + 32] = -slots[q, lo, p * 64 + 32:p * 64 + 64]
                turned[q, lo, p * 64 + 32:p * 64 + 64] = slots[q, lo, p * 64:p * 64 + 32]

    def product(i, q):
        rows = slice(q * 256, q * 256 + 256)
        direct = jnp.concatenate([slots[q, 0], slots[q, 1]], axis=1)
        crossed = jnp.concatenate([turned[q, 0], turned[q, 1]], axis=1)
        return jnp.dot(direct, wave_c[i, rows, :], preferred_element_type=jnp.float32) + jnp.dot(
            crossed, wave_s[i, rows, :], preferred_element_type=jnp.float32
        )

    regroup(0)
    replicas(0)
    regroup(1)
    replicas(1)
    regroup(2)
    regroup(3)
    replicas(2)
    replicas(3)
    collect(0)
    collect(1)
    for i in range(4):
        sums[i] = product(i, 0) + product(i, 1)
    collect(2)
    for i in range(4):
        sums[i] += product(i, 2)
    collect(3)

    for i in (3, 2, 1, 0):
        beam = sums[i] + product(i, 3)
        part[i] = jnp.sum(beam * beam, axis=0, keepdims=True) * (1.0 / (512.0 * 1024.0))

        def send():
            target = (f + 1 - core, z_partner(ahead + 4 * STEPS[i])[1][1])
            pltpu.make_async_remote_copy(
                part.at[i], recv_a.at[z], send_a, sem_a, device_id=target, device_id_type=MESH
            ).start()

        if i > 0:
            send()
        else:
            stays = jnp.logical_and(holds, core == 1)
            pl.when(jnp.logical_not(stays))(send)

            @pl.when(stays)
            def _():
                pltpu.make_async_copy(part.at[0], recv_a.at[z], sem_a).start()

    @pl.when(home)
    def _():
        pltpu.make_async_copy(recv_a, recv_a, sem_a).wait()
        total = recv_a[0]
        for b in range(1, BINS):
            total = total + recv_a[b]
        for b in range(BINS):
            out_b[b, :, :BLOCK] = recv_a[b]
            out_b[b, :, BLOCK:] = total
        for k in range(1, BINS):
            fo = lax.rem(f + k, BINS)
            pltpu.make_async_remote_copy(
                out_b.at[fo], recv_b.at[share], send_b, sem_b, device_id=(fo, g), device_id_type=MESH
            ).start()
        pltpu.make_async_copy(out_b.at[f], recv_b.at[share], sem_b).start()

    pltpu.make_async_copy(recv_b, recv_b, sem_b).wait()
    both = (recv_b[0] + recv_b[1]) + (recv_b[2] + recv_b[3])
    out_ref[...] = both

    @pl.when(holds)
    def _():
        for _ in range(3):
            pltpu.make_async_copy(points, points, points_send).wait()
        pltpu.make_async_copy(points.at[0:3], points.at[0:3], points_send).wait()

    @pl.when(home)
    def _():
        pltpu.make_async_copy(out_b.at[0:15], out_b.at[0:15], send_b).wait()

    pltpu.make_async_copy(part.at[0:3], part.at[0:3], send_a).wait()

    @pl.when(jnp.logical_not(jnp.logical_and(holds, core == 1)))
    def _():
        pltpu.make_async_copy(part.at[0], part.at[0], send_a).wait()

    pltpu.make_async_copy(send1.at[0:15], send1.at[0:15], send1_sem).wait()
    sent = wave_c.at[:, 0:7 * 32]
    pltpu.make_async_copy(sent, sent, send2_sem).wait()


def on_device(series, bins, sensor_coords, grid_coords):
    vmem = pltpu.VMEM
    bf16, f32 = jnp.bfloat16, jnp.float32
    dma = pltpu.SemaphoreType.DMA
    both = pl.pallas_call(
        kernel,
        out_shape=vmem((1, 2 * BLOCK), f32),
        in_specs=[pl.BlockSpec(memory_space=pltpu.HBM)] * 4,
        out_specs=pl.BlockSpec(memory_space=vmem),
        scratch_shapes=[
            pltpu.SMEM((BINS,), jnp.int32),
            vmem((3, CH), jnp.int32),
            vmem((3, BLOCK), jnp.int32),
            vmem((SNAP_LOC, CH_LOC, SAMP), bf16),
            vmem((2 * BINS, SAMP), bf16),
            vmem((CH, 128), bf16),
            vmem((CH, 128), bf16),
            vmem((4, 3, BLOCK), jnp.int32),
            vmem((2 * BINS, 8, 128), f32),
            vmem((BINS, 16, 128), bf16),
            vmem((ZS, 16, 128), bf16),
            vmem((4, 2, 256, 128), bf16),
            vmem((4, 2, 256, 128), bf16),
            vmem((4, CH, BLOCK), bf16),
            vmem((4, CH, BLOCK), bf16),
            vmem((4, 256, BLOCK), f32),
            vmem((4, 1, BLOCK), f32),
            vmem((BINS, 1, BLOCK), f32),
            vmem((BINS, 1, 2 * BLOCK), f32),
            vmem((4, 1, 2 * BLOCK), f32),
            dma, dma, dma, dma, dma, dma((4,)), dma, dma((4,)), dma, dma((4, 8)), dma, dma, dma, dma,
        ],
        compiler_params=pltpu.CompilerParams(
            collective_id=0, has_side_effects=True, vmem_limit_bytes=56 * 1024 * 1024
        ),
    )(bins, sensor_coords, grid_coords, series)
    return both[:, :BLOCK], both[0, BLOCK:] * (1.0 / BINS)


def solution(mesh):
    return jax.shard_map(
        on_device,
        mesh=mesh,
        in_specs=(P("freq", "grid", None), P(), P(), P(None, "grid")),
        out_specs=(P("freq", "grid"), P("grid")),
        check_vma=False,
    )
```

```python
import jax
import jax.numpy as jnp
from jax import lax
from jax.experimental import pallas as pl
from jax.experimental.pallas import tpu as pltpu
from jax.sharding import PartitionSpec as P

MESH = pl.DeviceIdType.MESH

SIN_COEF = (4.442883014678955, -7.308245658874512, 3.606354236602783, -0.8461116552352905, 0.1098245158791542)
COS_COEF = (1.4142135381698608, -6.978850841522217, 5.739460468292236, -1.883557915687561, 0.3106880187988281)

XS, ZS, BINS = 4, 16, 16
CH_LOC, SNAP_LOC, SAMP, BLOCK = 32, 32, 256, 256
CH = 1024
NEAR = (0, 1, 15, 2, 14, 3, 13, 4, 12, 5, 11, 6, 10, 7, 9, 8)
STEPS = (0, 3, 1, 2)


def horner(coef, z):
    acc = coef[-1] * z + coef[-2]
    for value in coef[-3::-1]:
        acc = acc * z + value
    return acc


def sincos_turns(turns):
    r = turns - jnp.round(turns)
    z = r * r
    s = horner(SIN_COEF, z) * r
    c = horner(COS_COEF, z)
    return 1.0 - s * s, s * c


def lattice(coords, flip):
    c = coords.astype(jnp.float32)
    norm = jnp.sum(c * c, axis=0, keepdims=True)
    high = jnp.floor(norm * (1.0 / 128.0)) * 128.0
    low = norm - high
    one = jnp.ones_like(norm)
    tail = (high, low, one, one) if flip else (one, one, high, low)
    scale = 1.0 if flip else -2.0
    zeros = jnp.zeros((9, c.shape[1]), jnp.float32)
    return jnp.concatenate([c * scale, *tail, zeros], axis=0)


def kernel(
    bins_hbm, sensor_hbm, grid_hbm, series_hbm, out_ref,
    bins_ref, sensor_ref, grid_ref, series_v, table_v, sensors_t, sensors_z, points, spec_f32,
    send1, recv1, slots, turned, wave_c, wave_s, sums, part, recv_a, out_b, recv_b,
    bins_sem, sensor_sem, grid_sem, series_sem, points_send, points_recv, send1_sem, recv1_sem, send2_sem, recv2_sem,
    send_a, sem_a, send_b, sem_b,
):
    f = lax.axis_index("freq")
    g = lax.axis_index("grid")
    core, x, y_hi = lax.rem(f, 2), lax.rem(f // 2, XS), f // (2 * XS)
    x_hi, x_lo = x // 2, lax.rem(x, 2)
    z, y_lo = lax.rem(g, ZS), g // ZS
    pos = x_lo * 2 + core
    own8 = pos * 2 + y_lo
    share = x_hi * 2 + y_hi
    ahead = lax.rem((1 - core) * 2 + 1 - x_lo + ZS - z, 4)
    holds = ahead == 0
    home = jnp.logical_and(core == 1, lax.rem(z, 2) != x_lo)

    def group_member(k):
        other = lax.rem(own8 + k, 8)
        lo, place = lax.rem(other, 2), other // 2
        xo = x_hi * 2 + place // 2
        return lo, place, ((y_hi * XS + xo) * 2 + lax.rem(place, 2), lo * ZS + z)

    def z_partner(k):
        zo = lax.rem(z + k, ZS)
        return zo, (f, y_lo * ZS + zo)

    loads = [
        pltpu.make_async_copy(*pair)
        for pair in (
            (bins_hbm, bins_ref, bins_sem),
            (series_hbm, series_v, series_sem),
            (grid_hbm, grid_ref, grid_sem),
            (sensor_hbm, sensor_ref, sensor_sem),
        )
    ]
    for load in loads:
        load.start()

    barrier = pltpu.get_barrier_semaphore()
    for k in NEAR[:0:-1]:
        pl.semaphore_signal(barrier, inc=1, device_id=z_partner(k)[1], device_id_type=MESH)
    for k in range(1, 4):
        other = lax.rem(share + k, 4)
        for place in range(4):
            fo = (lax.rem(other, 2) * XS + (other // 2) * 2 + place // 2) * 2 + place % 2
            pl.semaphore_signal(barrier, inc=1, device_id=(fo, g), device_id_type=MESH)
    for k in range(1, 8):
        pl.semaphore_signal(barrier, inc=1, device_id=group_member(k)[2], device_id_type=MESH)

    loads[0].wait()
    row = lax.broadcasted_iota(jnp.int32, (2 * BINS, SAMP), 0)
    time = lax.broadcasted_iota(jnp.int32, (2 * BINS, SAMP), 1)
    number = jnp.zeros((2 * BINS, SAMP), jnp.int32)
    for b in range(BINS):
        number = jnp.where(row // 2 == b, bins_ref[b], number)
    cycles = (number * time + (row % 2) * (SAMP // 4)) & (SAMP - 1)
    table_v[...] = (sincos_turns(cycles.astype(jnp.float32) * (1.0 / SAMP))[0] * (SAMP / 2.0) ** -0.5).astype(
        jnp.bfloat16
    )

    loads[1].wait()
    spec = lax.dot_general(
        table_v[...], series_v[...].reshape(SNAP_LOC * CH_LOC, SAMP),
        (((1,), (1,)), ((), ())), preferred_element_type=jnp.float32,
    )
    for t in range(8):
        spec_f32[:, t, :] = spec[:, t * 128:(t + 1) * 128]
    send1[...] = spec_f32[...].reshape(BINS, 16, 128).astype(jnp.bfloat16)

    loads[3].wait()
    sensors_t[...] = jnp.transpose(
        jnp.concatenate([lattice(sensor_ref[...], True), jnp.zeros((112, CH), jnp.float32)], axis=0)
    ).astype(jnp.bfloat16)
    for p in range(ZS):
        for lo in range(2):
            start = pl.multiple_of((lo * ZS + lax.rem(z + NEAR[p], ZS)) * CH_LOC, CH_LOC)
            to = (2 * (p // 4) + lo) * 128 + (p % 4) * CH_LOC
            sensors_z[to:to + CH_LOC, :] = sensors_t[pl.ds(start, CH_LOC), :]
    rate = bins_ref[z].astype(jnp.float32) * (1.0 / 128.0)

    pl.semaphore_wait(barrier, ZS - 1 + 12 + 7)

    for k in NEAR[1:]:
        zo, device = z_partner(k)
        place = NEAR.index(ZS - k)
        pltpu.make_async_remote_copy(
            send1.at[zo], recv1.at[place], send1_sem, recv1_sem.at[place // 4], device_id=device, device_id_type=MESH
        ).start()
    pltpu.make_async_copy(send1.at[z], recv1.at[0], recv1_sem.at[0]).start()

    @pl.when(holds)
    def _():
        loads[2].wait()
        for k in NEAR[1:]:
            slot = STEPS.index((ZS - k) // 4)
            pltpu.make_async_remote_copy(
                grid_ref, points.at[slot], points_send, points_recv.at[slot],
                device_id=z_partner(k)[1], device_id_type=MESH,
            ).start()
        pltpu.make_async_copy(grid_ref, points.at[0], points_recv.at[0]).start()

    @pl.when(jnp.logical_not(holds))
    def _():
        loads[2].wait()

    def replicas(i):
        pltpu.make_async_copy(points.at[i], points.at[i], points_recv.at[i]).wait()
        rhs = lattice(points[i], False).astype(jnp.bfloat16)

        def body(n, carry):
            rows = pl.ds(pl.multiple_of(n * 128, 128), 128)
            squared = jnp.dot(sensors_z[rows, :16], rhs, preferred_element_type=jnp.float32)
            root = lax.rsqrt(jnp.maximum(squared, 0.5))
            c, s = sincos_turns((squared * rate) * root)
            wave_c[i, rows, :] = c.astype(jnp.bfloat16)
            wave_s[i, rows, :] = s.astype(jnp.bfloat16)
            return carry

        lax.fori_loop(0, CH // 128, body, 0)

    lane = lax.broadcasted_iota(jnp.int32, (16, 128), 1) // 32

    def regroup(q):
        four = recv1.at[4 * q:4 * q + 4]
        pltpu.make_async_copy(four, four, recv1_sem.at[q]).wait()
        pieces = [recv1[4 * q + j].astype(jnp.float32) for j in range(4)]
        tiles = []
        for h in range(4):
            tile = None
            for j in range(4):
                shift = ((j - h) * 32) % 128
                moved = pieces[j] if shift == 0 else pltpu.roll(pieces[j], shift, 1)
                tile = moved if tile is None else jnp.where(lane == j, moved, tile)
            tiles.append(tile)
        stacked = jnp.concatenate([t[:8] for t in tiles] + [t[8:] for t in tiles], axis=0)
        mine = pl.ds(pl.multiple_of(pos * 64, 64), 64)
        slots[q, y_lo, mine, :] = stacked.astype(jnp.bfloat16)
        block = slots.at[q, y_lo, mine]
        for k in range(1, 8):
            pltpu.make_async_remote_copy(
                block, block, send2_sem, recv2_sem.at[q, own8],
                device_id=group_member(k)[2], device_id_type=MESH,
            ).start()

    def collect(q):
        for k in range(1, 8):
            lo, place, _ = group_member(k)
            block = slots.at[q, lo, pl.ds(pl.multiple_of(place * 64, 64), 64)]
            pltpu.make_async_copy(block, block, recv2_sem.at[q, lax.rem(own8 + k, 8)]).wait()
        for lo in range(2):
            for p in range(4):
                turned[q, lo, p * 64:p * 64 + 32] = -slots[q, lo, p * 64 + 32:p * 64 + 64]
                turned[q, lo, p * 64 + 32:p * 64 + 64] = slots[q, lo, p * 64:p * 64 + 32]

    def product(i, q):
        rows = slice(q * 256, q * 256 + 256)
        direct = jnp.concatenate([slots[q, 0], slots[q, 1]], axis=1)
        crossed = jnp.concatenate([turned[q, 0], turned[q, 1]], axis=1)
        return jnp.dot(direct, wave_c[i, rows, :], preferred_element_type=jnp.float32) + jnp.dot(
            crossed, wave_s[i, rows, :], preferred_element_type=jnp.float32
        )

    regroup(0)
    replicas(0)
    regroup(1)
    replicas(1)
    regroup(2)
    regroup(3)
    replicas(2)
    replicas(3)
    collect(0)
    collect(1)
    for i in range(4):
        sums[i] = product(i, 0) + product(i, 1)
    collect(2)
    for i in range(4):
        sums[i] += product(i, 2)
    collect(3)

    for i in (3, 2, 1, 0):
        beam = sums[i] + product(i, 3)
        part[i] = jnp.sum(beam * beam, axis=0, keepdims=True) * (1.0 / (512.0 * 1024.0))

        def send():
            target = (f + 1 - core, z_partner(ahead + 4 * STEPS[i])[1][1])
            pltpu.make_async_remote_copy(
                part.at[i], recv_a.at[z], send_a, sem_a, device_id=target, device_id_type=MESH
            ).start()

        if i > 0:
            send()
        else:
            stays = jnp.logical_and(holds, core == 1)
            pl.when(jnp.logical_not(stays))(send)

            @pl.when(stays)
            def _():
                pltpu.make_async_copy(part.at[0], recv_a.at[z], sem_a).start()

    @pl.when(home)
    def _():
        pltpu.make_async_copy(recv_a, recv_a, sem_a).wait()
        total = recv_a[0]
        for b in range(1, BINS):
            total = total + recv_a[b]
        for b in range(BINS):
            out_b[b, :, :BLOCK] = recv_a[b]
            out_b[b, :, BLOCK:] = total
        for k in (14, 10, 6, 2, 12, 4, 8, 13, 11, 5, 3, 9, 7, 15, 1):
            fo = lax.rem(f + k, BINS)
            pltpu.make_async_remote_copy(
                out_b.at[fo], recv_b.at[share], send_b, sem_b, device_id=(fo, g), device_id_type=MESH
            ).start()
        pltpu.make_async_copy(out_b.at[f], recv_b.at[share], sem_b).start()

    pltpu.make_async_copy(recv_b, recv_b, sem_b).wait()
    both = (recv_b[0] + recv_b[1]) + (recv_b[2] + recv_b[3])
    out_ref[...] = both

    @pl.when(holds)
    def _():
        for _ in range(3):
            pltpu.make_async_copy(points, points, points_send).wait()
        pltpu.make_async_copy(points.at[0:3], points.at[0:3], points_send).wait()

    @pl.when(home)
    def _():
        pltpu.make_async_copy(out_b.at[0:15], out_b.at[0:15], send_b).wait()

    pltpu.make_async_copy(part.at[0:3], part.at[0:3], send_a).wait()

    @pl.when(jnp.logical_not(jnp.logical_and(holds, core == 1)))
    def _():
        pltpu.make_async_copy(part.at[0], part.at[0], send_a).wait()

    pltpu.make_async_copy(send1.at[0:15], send1.at[0:15], send1_sem).wait()
    sent = wave_c.at[:, 0:7 * 32]
    pltpu.make_async_copy(sent, sent, send2_sem).wait()


def on_device(series, bins, sensor_coords, grid_coords):
    vmem = pltpu.VMEM
    bf16, f32 = jnp.bfloat16, jnp.float32
    dma = pltpu.SemaphoreType.DMA
    both = pl.pallas_call(
        kernel,
        out_shape=vmem((1, 2 * BLOCK), f32),
        in_specs=[pl.BlockSpec(memory_space=pltpu.HBM)] * 4,
        out_specs=pl.BlockSpec(memory_space=vmem),
        scratch_shapes=[
            pltpu.SMEM((BINS,), jnp.int32),
            vmem((3, CH), jnp.int32),
            vmem((3, BLOCK), jnp.int32),
            vmem((SNAP_LOC, CH_LOC, SAMP), bf16),
            vmem((2 * BINS, SAMP), bf16),
            vmem((CH, 128), bf16),
            vmem((CH, 128), bf16),
            vmem((4, 3, BLOCK), jnp.int32),
            vmem((2 * BINS, 8, 128), f32),
            vmem((BINS, 16, 128), bf16),
            vmem((ZS, 16, 128), bf16),
            vmem((4, 2, 256, 128), bf16),
            vmem((4, 2, 256, 128), bf16),
            vmem((4, CH, BLOCK), bf16),
            vmem((4, CH, BLOCK), bf16),
            vmem((4, 256, BLOCK), f32),
            vmem((4, 1, BLOCK), f32),
            vmem((BINS, 1, BLOCK), f32),
            vmem((BINS, 1, 2 * BLOCK), f32),
            vmem((4, 1, 2 * BLOCK), f32),
            dma, dma, dma, dma, dma, dma((4,)), dma, dma((4,)), dma, dma((4, 8)), dma, dma, dma, dma,
        ],
        compiler_params=pltpu.CompilerParams(
            collective_id=0, has_side_effects=True, vmem_limit_bytes=56 * 1024 * 1024
        ),
    )(bins, sensor_coords, grid_coords, series)
    return both[:, :BLOCK], both[0, BLOCK:] * (1.0 / BINS)


def solution(mesh):
    return jax.shard_map(
        on_device,
        mesh=mesh,
        in_specs=(P("freq", "grid", None), P(), P(), P(None, "grid")),
        out_specs=(P("freq", "grid"), P("grid")),
        check_vma=False,
    )
```

```python
import jax
import jax.numpy as jnp
from jax import lax
from jax.experimental import pallas as pl
from jax.experimental.pallas import tpu as pltpu
from jax.sharding import PartitionSpec as P

MESH = pl.DeviceIdType.MESH

SIN_COEF = (4.442883014678955, -7.308245658874512, 3.606354236602783, -0.8461116552352905, 0.1098245158791542)
COS_COEF = (1.4142135381698608, -6.978850841522217, 5.739460468292236, -1.883557915687561, 0.3106880187988281)

XS, ZS, BINS = 4, 16, 16
CH_LOC, SNAP_LOC, SAMP, BLOCK = 32, 32, 256, 256
CH = 1024
NEAR = (0, 1, 15, 2, 14, 3, 13, 4, 12, 5, 11, 6, 10, 7, 9, 8)
STEPS = (0, 3, 1, 2)


def horner(coef, z):
    acc = coef[-1] * z + coef[-2]
    for value in coef[-3::-1]:
        acc = acc * z + value
    return acc


def sincos_turns(turns):
    r = turns - jnp.round(turns)
    z = r * r
    s = horner(SIN_COEF, z) * r
    c = horner(COS_COEF, z)
    return 1.0 - s * s, s * c


def lattice(coords, flip):
    c = coords.astype(jnp.float32)
    norm = jnp.sum(c * c, axis=0, keepdims=True)
    high = jnp.floor(norm * (1.0 / 128.0)) * 128.0
    low = norm - high
    one = jnp.ones_like(norm)
    tail = (high, low, one, one) if flip else (one, one, high, low)
    scale = 1.0 if flip else -2.0
    zeros = jnp.zeros((9, c.shape[1]), jnp.float32)
    return jnp.concatenate([c * scale, *tail, zeros], axis=0)


def kernel(
    bins_hbm, sensor_hbm, grid_hbm, series_hbm, out_ref,
    bins_ref, sensor_ref, grid_ref, series_v, table_v, sensors_t, sensors_z, points, spec_f32,
    send1, recv1, slots, turned, wave_c, wave_s, sums, part, recv_a, out_b, recv_b,
    bins_sem, sensor_sem, grid_sem, series_sem, points_send, points_recv, send1_sem, recv1_sem, send2_sem, recv2_sem,
    send_a, sem_a, send_b, sem_b,
):
    f = lax.axis_index("freq")
    g = lax.axis_index("grid")
    core, x, y_hi = lax.rem(f, 2), lax.rem(f // 2, XS), f // (2 * XS)
    x_hi, x_lo = x // 2, lax.rem(x, 2)
    z, y_lo = lax.rem(g, ZS), g // ZS
    pos = x_lo * 2 + core
    own8 = pos * 2 + y_lo
    share = x_hi * 2 + y_hi
    ahead = lax.rem((1 - core) * 2 + 1 - x_lo + ZS - z, 4)
    holds = ahead == 0
    home = jnp.logical_and(core == 1, lax.rem(z, 2) != x_lo)

    def group_member(k):
        other = lax.rem(own8 + k, 8)
        lo, place = lax.rem(other, 2), other // 2
        xo = x_hi * 2 + place // 2
        return lo, place, ((y_hi * XS + xo) * 2 + lax.rem(place, 2), lo * ZS + z)

    def z_partner(k):
        zo = lax.rem(z + k, ZS)
        return zo, (f, y_lo * ZS + zo)

    loads = [
        pltpu.make_async_copy(*pair)
        for pair in (
            (bins_hbm, bins_ref, bins_sem),
            (series_hbm, series_v, series_sem),
            (grid_hbm, grid_ref, grid_sem),
            (sensor_hbm, sensor_ref, sensor_sem),
        )
    ]
    for load in loads:
        load.start()

    barrier = pltpu.get_barrier_semaphore()
    for k in NEAR[:0:-1]:
        pl.semaphore_signal(barrier, inc=1, device_id=z_partner(k)[1], device_id_type=MESH)
    for k in range(1, 4):
        other = lax.rem(share + k, 4)
        for place in range(4):
            fo = (lax.rem(other, 2) * XS + (other // 2) * 2 + place // 2) * 2 + place % 2
            pl.semaphore_signal(barrier, inc=1, device_id=(fo, g), device_id_type=MESH)
    for k in range(1, 8):
        pl.semaphore_signal(barrier, inc=1, device_id=group_member(k)[2], device_id_type=MESH)

    loads[0].wait()
    row = lax.broadcasted_iota(jnp.int32, (2 * BINS, SAMP), 0)
    time = lax.broadcasted_iota(jnp.int32, (2 * BINS, SAMP), 1)
    number = jnp.zeros((2 * BINS, SAMP), jnp.int32)
    for b in range(BINS):
        number = jnp.where(row // 2 == b, bins_ref[b], number)
    cycles = (number * time + (row % 2) * (SAMP // 4)) & (SAMP - 1)
    table_v[...] = (sincos_turns(cycles.astype(jnp.float32) * (1.0 / SAMP))[0] * (SAMP / 2.0) ** -0.5).astype(
        jnp.bfloat16
    )

    loads[1].wait()
    spec = lax.dot_general(
        table_v[...], series_v[...].reshape(SNAP_LOC * CH_LOC, SAMP),
        (((1,), (1,)), ((), ())), preferred_element_type=jnp.float32,
    )
    for t in range(8):
        spec_f32[:, t, :] = spec[:, t * 128:(t + 1) * 128]
    send1[...] = spec_f32[...].reshape(BINS, 16, 128).astype(jnp.bfloat16)

    loads[3].wait()
    sensors_t[...] = jnp.transpose(
        jnp.concatenate([lattice(sensor_ref[...], True), jnp.zeros((112, CH), jnp.float32)], axis=0)
    ).astype(jnp.bfloat16)
    for p in range(ZS):
        for lo in range(2):
            start = pl.multiple_of((lo * ZS + lax.rem(z + NEAR[p], ZS)) * CH_LOC, CH_LOC)
            to = (2 * (p // 4) + lo) * 128 + (p % 4) * CH_LOC
            sensors_z[to:to + CH_LOC, :] = sensors_t[pl.ds(start, CH_LOC), :]
    rate = bins_ref[z].astype(jnp.float32) * (1.0 / 128.0)

    pl.semaphore_wait(barrier, ZS - 1 + 12 + 7)

    for k in NEAR[1:]:
        zo, device = z_partner(k)
        place = NEAR.index(ZS - k)
        pltpu.make_async_remote_copy(
            send1.at[zo], recv1.at[place], send1_sem, recv1_sem.at[place // 4], device_id=device, device_id_type=MESH
        ).start()
    pltpu.make_async_copy(send1.at[z], recv1.at[0], recv1_sem.at[0]).start()

    @pl.when(holds)
    def _():
        loads[2].wait()
        for k in NEAR[1:]:
            slot = STEPS.index((ZS - k) // 4)
            pltpu.make_async_remote_copy(
                grid_ref, points.at[slot], points_send, points_recv.at[slot],
                device_id=z_partner(k)[1], device_id_type=MESH,
            ).start()
        pltpu.make_async_copy(grid_ref, points.at[0], points_recv.at[0]).start()

    @pl.when(jnp.logical_not(holds))
    def _():
        loads[2].wait()

    def replicas(i):
        pltpu.make_async_copy(points.at[i], points.at[i], points_recv.at[i]).wait()
        rhs = lattice(points[i], False).astype(jnp.bfloat16)

        def body(n, carry):
            rows = pl.ds(pl.multiple_of(n * 128, 128), 128)
            squared = jnp.dot(sensors_z[rows, :16], rhs, preferred_element_type=jnp.float32)
            root = lax.rsqrt(jnp.maximum(squared, 0.5))
            c, s = sincos_turns((squared * rate) * root)
            wave_c[i, rows, :] = c.astype(jnp.bfloat16)
            wave_s[i, rows, :] = s.astype(jnp.bfloat16)
            return carry

        lax.fori_loop(0, CH // 128, body, 0)

    lane = lax.broadcasted_iota(jnp.int32, (16, 128), 1) // 32

    def regroup(q):
        four = recv1.at[4 * q:4 * q + 4]
        pltpu.make_async_copy(four, four, recv1_sem.at[q]).wait()
        pieces = [recv1[4 * q + j].astype(jnp.float32) for j in range(4)]
        tiles = []
        for h in range(4):
            tile = None
            for j in range(4):
                shift = ((j - h) * 32) % 128
                moved = pieces[j] if shift == 0 else pltpu.roll(pieces[j], shift, 1)
                tile = moved if tile is None else jnp.where(lane == j, moved, tile)
            tiles.append(tile)
        stacked = jnp.concatenate([t[:8] for t in tiles] + [t[8:] for t in tiles], axis=0)
        mine = pl.ds(pl.multiple_of(pos * 64, 64), 64)
        slots[q, y_lo, mine, :] = stacked.astype(jnp.bfloat16)
        block = slots.at[q, y_lo, mine]
        for k in range(1, 8):
            pltpu.make_async_remote_copy(
                block, block, send2_sem, recv2_sem.at[q, own8],
                device_id=group_member(k)[2], device_id_type=MESH,
            ).start()

    def collect(q):
        for k in range(1, 8):
            lo, place, _ = group_member(k)
            block = slots.at[q, lo, pl.ds(pl.multiple_of(place * 64, 64), 64)]
            pltpu.make_async_copy(block, block, recv2_sem.at[q, lax.rem(own8 + k, 8)]).wait()
        for lo in range(2):
            for p in range(4):
                turned[q, lo, p * 64:p * 64 + 32] = -slots[q, lo, p * 64 + 32:p * 64 + 64]
                turned[q, lo, p * 64 + 32:p * 64 + 64] = slots[q, lo, p * 64:p * 64 + 32]

    def product(i, q):
        rows = slice(q * 256, q * 256 + 256)
        direct = jnp.concatenate([slots[q, 0], slots[q, 1]], axis=1)
        crossed = jnp.concatenate([turned[q, 0], turned[q, 1]], axis=1)
        return jnp.dot(direct, wave_c[i, rows, :], preferred_element_type=jnp.float32) + jnp.dot(
            crossed, wave_s[i, rows, :], preferred_element_type=jnp.float32
        )

    regroup(0)
    replicas(0)
    regroup(1)
    replicas(1)
    regroup(2)
    regroup(3)
    replicas(2)
    replicas(3)
    collect(0)
    collect(1)
    for i in range(4):
        sums[i] = product(i, 0) + product(i, 1)
    collect(2)
    for i in range(4):
        sums[i] += product(i, 2)
    collect(3)

    for i in (3, 2, 1, 0):
        beam = sums[i] + product(i, 3)
        part[i] = jnp.sum(beam * beam, axis=0, keepdims=True) * (1.0 / (512.0 * 1024.0))

        def send():
            target = (f + 1 - core, z_partner(ahead + 4 * STEPS[i])[1][1])
            pltpu.make_async_remote_copy(
                part.at[i], recv_a.at[z], send_a, sem_a, device_id=target, device_id_type=MESH
            ).start()

        if i > 0:
            send()
        else:
            stays = jnp.logical_and(holds, core == 1)
            pl.when(jnp.logical_not(stays))(send)

            @pl.when(stays)
            def _():
                pltpu.make_async_copy(part.at[0], recv_a.at[z], sem_a).start()

    @pl.when(home)
    def _():
        pltpu.make_async_copy(recv_a, recv_a, sem_a).wait()
        terms = [recv_a[b] for b in range(BINS)]
        while len(terms) > 1:
            terms = [left + right for left, right in zip(terms[::2], terms[1::2])]
        total = terms[0]
        for b in range(BINS):
            out_b[b, :, :BLOCK] = recv_a[b]
            out_b[b, :, BLOCK:] = total
        for k in (14, 10, 6, 2, 12, 4, 8, 13, 11, 5, 3, 9, 7, 15, 1):
            fo = lax.rem(f + k, BINS)
            pltpu.make_async_remote_copy(
                out_b.at[fo], recv_b.at[share], send_b, sem_b, device_id=(fo, g), device_id_type=MESH
            ).start()
        pltpu.make_async_copy(out_b.at[f], recv_b.at[share], sem_b).start()

    pltpu.make_async_copy(recv_b, recv_b, sem_b).wait()
    both = (recv_b[0] + recv_b[1]) + (recv_b[2] + recv_b[3])
    out_ref[...] = both

    @pl.when(holds)
    def _():
        for _ in range(3):
            pltpu.make_async_copy(points, points, points_send).wait()
        pltpu.make_async_copy(points.at[0:3], points.at[0:3], points_send).wait()

    @pl.when(home)
    def _():
        pltpu.make_async_copy(out_b.at[0:15], out_b.at[0:15], send_b).wait()

    pltpu.make_async_copy(part.at[0:3], part.at[0:3], send_a).wait()

    @pl.when(jnp.logical_not(jnp.logical_and(holds, core == 1)))
    def _():
        pltpu.make_async_copy(part.at[0], part.at[0], send_a).wait()

    pltpu.make_async_copy(send1.at[0:15], send1.at[0:15], send1_sem).wait()
    sent = wave_c.at[:, 0:7 * 32]
    pltpu.make_async_copy(sent, sent, send2_sem).wait()


def on_device(series, bins, sensor_coords, grid_coords):
    vmem = pltpu.VMEM
    bf16, f32 = jnp.bfloat16, jnp.float32
    dma = pltpu.SemaphoreType.DMA
    both = pl.pallas_call(
        kernel,
        out_shape=vmem((1, 2 * BLOCK), f32),
        in_specs=[pl.BlockSpec(memory_space=pltpu.HBM)] * 4,
        out_specs=pl.BlockSpec(memory_space=vmem),
        scratch_shapes=[
            pltpu.SMEM((BINS,), jnp.int32),
            vmem((3, CH), jnp.int32),
            vmem((3, BLOCK), jnp.int32),
            vmem((SNAP_LOC, CH_LOC, SAMP), bf16),
            vmem((2 * BINS, SAMP), bf16),
            vmem((CH, 128), bf16),
            vmem((CH, 128), bf16),
            vmem((4, 3, BLOCK), jnp.int32),
            vmem((2 * BINS, 8, 128), f32),
            vmem((BINS, 16, 128), bf16),
            vmem((ZS, 16, 128), bf16),
            vmem((4, 2, 256, 128), bf16),
            vmem((4, 2, 256, 128), bf16),
            vmem((4, CH, BLOCK), bf16),
            vmem((4, CH, BLOCK), bf16),
            vmem((4, 256, BLOCK), f32),
            vmem((4, 1, BLOCK), f32),
            vmem((BINS, 1, BLOCK), f32),
            vmem((BINS, 1, 2 * BLOCK), f32),
            vmem((4, 1, 2 * BLOCK), f32),
            dma, dma, dma, dma, dma, dma((4,)), dma, dma((4,)), dma, dma((4, 8)), dma, dma, dma, dma,
        ],
        compiler_params=pltpu.CompilerParams(
            collective_id=0, has_side_effects=True, vmem_limit_bytes=56 * 1024 * 1024
        ),
    )(bins, sensor_coords, grid_coords, series)
    return both[:, :BLOCK], both[0, BLOCK:] * (1.0 / BINS)


def solution(mesh):
    return jax.shard_map(
        on_device,
        mesh=mesh,
        in_specs=(P("freq", "grid", None), P(), P(), P(None, "grid")),
        out_specs=(P("freq", "grid"), P("grid")),
        check_vma=False,
    )
```
